32 devices in a mesh: vocab: 16 (over z, y, x), hid: 2 (over core).
Axes of the slice: x: 2, y: 2, z: 4, core: 2. Of those that a mesh axis runs over, the one named last changes fastest.
Arguments:
- hidden_states: bfloat16 [768, 8192], P('vocab', 'hid'), may hold values from -10 to 10
- head_weight: bfloat16 [8192, 20480], P('hid', 'vocab'), may hold values from -8 to 8
- focus_tiles: int32 [256, 2], P('vocab'), may hold values from 0 to 191, as said below
- focus_blocks: bfloat16 [256, 128, 128], P('vocab'), may hold values from -0.5 to 0.5
Outputs:
- student_target: float32 [768, 24576], P('hid', 'vocab')
The draws below stay inside these ranges and needn't reach their ends.
Inputs may be any that keep to these rules, and one draw needn't show every extreme that they name: `focus_tiles`: rows k * 16 to (k + 1) * 16 - 1 name teacher tiles k * 10 to (k + 1) * 10 - 1 in column 0; column 1 is a student tile, whose owner is the tile divided by 12. Within each such block of rows no owner is named more than 2 times, and one owner, drawn from the seed, is named exactly 2 times in every block; other owners may be named 2 times as well.
All inputs are finite; a program needn't handle non-finite values.
Results may differ from the reference program's by a relative error of at most 0.0035.
Values may be sent and summed in bfloat16 or wider, within the bound.
No kernel may reach another device: no remote copies, remote signals or barrier semaphores. Data moves between devices by JAX's collectives and lax.ppermute only.
A program may use at most 64 MiB of HBM per device.

```python
import math
import jax
import jax.numpy as jnp
from jax import lax

D = 8192
TILE = 128
TILES_DEV = 10
STILES_DEV = 12
CAP = 2
P_SIZE = 768
NNZ_DEV = 16
V = 20480
S = 24576
NNZ = 256


def draw_hidden_states(key, part):
    noise_part = jnp.clip(jax.random.normal(jax.random.fold_in(key, 11), (P_SIZE, D), jnp.float32), -3.0, 3.0)
    row_scale = jnp.exp(jax.random.uniform(jax.random.fold_in(key, 29), (P_SIZE, 1), jnp.float32, math.log(0.1), 0.0))
    return (noise_part * row_scale).astype(jnp.bfloat16)


def draw_head_weight(key, part):
    noise_part = 3.0 / math.sqrt(D) * jnp.clip(jax.random.normal(jax.random.fold_in(key, 13), (D, V), jnp.float32), -4.0, 4.0)
    return noise_part.astype(jnp.bfloat16)


def draw_focus_tiles(key, part):
    senders = NNZ // NNZ_DEV
    hot_key, perm_key, teacher_key, student_key = jax.random.split(key, 4)
    hottest = jax.random.randint(hot_key, (), 0, senders)
    other_count = NNZ_DEV - CAP
    half_count = (other_count + 1) // 2

    def one_sender(sub_key):
        shuffle_key = jax.random.fold_in(sub_key, 101)
        chosen = jax.random.permutation(jax.random.fold_in(sub_key, 3), senders - 1)[:half_count]
        others = jnp.concatenate([chosen, chosen])[:other_count]
        others = others + (others >= hottest).astype(jnp.int32)
        owners = jnp.concatenate([jnp.full((CAP,), hottest, jnp.int32), others.astype(jnp.int32)])
        return owners[jax.random.permutation(shuffle_key, NNZ_DEV)]
    owners = jax.vmap(one_sender)(jax.random.split(perm_key, senders))
    sender_index = jnp.arange(senders, dtype=jnp.int32)[:, None]
    teacher = jax.random.randint(teacher_key, (senders, NNZ_DEV), 0, TILES_DEV) + sender_index * TILES_DEV
    student = owners * STILES_DEV + jax.random.randint(student_key, (senders, NNZ_DEV), 0, STILES_DEV)
    return jnp.stack([teacher, student], axis=-1).reshape(NNZ, 2).astype(jnp.int32)


def level_of(stream_key, extent, pieces, low, high):
    loudness = 1.0
    for dim, shards_of in pieces:
        steps = jax.random.uniform(jax.random.fold_in(jax.random.fold_in(stream_key, 6), dim), (shards_of,), jnp.float32, low / len(pieces), high / len(pieces))
        loudness = loudness * jnp.repeat(jnp.exp(steps), extent[dim] // shards_of).reshape((-1,) + (1,) * (len(extent) - 1 - dim))
    return loudness


def centred(stream_key, shape, width, limit, cuts=(), held_as=jnp.bfloat16):
    level = level_of(stream_key, shape, cuts, -0.22, 0.18) if cuts else 1.0
    array = jax.random.normal(stream_key, shape, jnp.float32) * width * level
    return jnp.minimum(jnp.maximum(array, -limit), limit).astype(held_as)


def setup_inputs(seed: int = 0) -> dict:
    keys = jax.random.split(jax.random.key(seed), 5)
    hidden_states = draw_hidden_states(jax.random.fold_in(keys[4], 71), 0)
    head_weight = draw_head_weight(jax.random.fold_in(keys[4], 71), 0)
    focus_tiles = draw_focus_tiles(jax.random.fold_in(keys[4], 71), 0)
    focus_blocks = centred(keys[3], (NNZ, TILE, TILE), TILE ** -0.5, 0.5, ((0, 16),))
    return {"hidden_states": hidden_states, "head_weight": head_weight, "focus_tiles": focus_tiles, "focus_blocks": focus_blocks}


def reference(hidden_states, head_weight, focus_tiles, focus_blocks):
    logits = jnp.dot(hidden_states, head_weight, preferred_element_type=jnp.float32)
    row_top = jnp.max(logits, axis=1, keepdims=True)
    exp_values = jnp.exp(logits - row_top)
    row_sum = jnp.sum(exp_values, axis=1, keepdims=True)
    weights = exp_values.astype(jnp.bfloat16)
    row_count = weights.shape[0]
    prob_tiles = weights.reshape(row_count, V // TILE, TILE)

    def add_entry(accumulator, entry_pair):
        coordinate, focus_block = entry_pair
        prob_tile = lax.dynamic_index_in_dim(prob_tiles, coordinate[0].astype(jnp.int32), 1, keepdims=False)
        term_rows = jnp.dot(prob_tile, focus_block, preferred_element_type=jnp.float32)
        previous = lax.dynamic_index_in_dim(accumulator, coordinate[1].astype(jnp.int32), 1, keepdims=False)
        accumulator = lax.dynamic_update_index_in_dim(accumulator, previous + term_rows, coordinate[1].astype(jnp.int32), 1)
        return accumulator, None

    accumulator = jnp.zeros((row_count, S // TILE, TILE), jnp.float32)
    accumulator, _ = lax.scan(add_entry, accumulator, (focus_tiles, focus_blocks))
    mapped = accumulator.reshape(row_count, S)
    return S * mapped / row_sum
```

```python
import functools

import jax
import jax.numpy as jnp
from jax import lax
from jax.experimental import pallas as pl
from jax.experimental.pallas import tpu as pltpu
from jax.sharding import PartitionSpec as P

TILE = 128
STILES_DEV = 12
CAP = 2
VMEM = pl.BlockSpec(memory_space=pltpu.VMEM)
SMEM = pl.BlockSpec(memory_space=pltpu.SMEM)


def map_kernel(blocks, plan_ref, kept_ref, came_ref, focus_ref, out_ref, stat_ref, tiles_ref):
    rows = kept_ref.shape[0] // blocks
    turn = plan_ref[2, 0]
    for i in range(blocks):
        source = pl.ds(pl.multiple_of((turn ^ i) * rows, 8), rows)
        target = pl.ds(i * rows, rows)
        logits = kept_ref[source, :] + came_ref[source, :]
        top = jnp.max(logits, axis=1, keepdims=True)
        values = jnp.exp(logits - top)
        total = jnp.sum(values, axis=1, keepdims=True)
        lane = lax.broadcasted_iota(jnp.int32, (rows, TILE), 1)
        stat_ref[target, :] = jnp.where(lane == 0, top, total)
        weights = values.astype(jnp.bfloat16)
        for t in range(tiles_ref.shape[0]):
            tiles_ref[t, target, :] = weights[:, t * TILE : (t + 1) * TILE]

    @pl.loop(0, focus_ref.shape[0])
    def _(e):
        term = jnp.dot(
            tiles_ref[plan_ref[0, e]], focus_ref[e], preferred_element_type=jnp.float32
        )
        out_ref[plan_ref[1, e]] = term.astype(jnp.bfloat16)


def map_rows(plan, kept, came, focus_blocks, slots, blocks):
    rows, columns = kept.shape
    entries = focus_blocks.shape[0]
    return pl.pallas_call(
        functools.partial(map_kernel, blocks),
        out_shape=(
            jax.ShapeDtypeStruct((slots, rows, TILE), jnp.bfloat16),
            jax.ShapeDtypeStruct((rows, TILE), jnp.float32),
        ),
        in_specs=[SMEM, VMEM, VMEM, VMEM],
        out_specs=(VMEM, VMEM),
        scratch_shapes=[pltpu.VMEM((columns // TILE, rows, TILE), jnp.bfloat16)],
        compiler_params=pltpu.CompilerParams(vmem_limit_bytes=32 << 20),
        cost_estimate=pl.CostEstimate(
            flops=2 * entries * rows * TILE * TILE,
            bytes_accessed=8 * rows * columns + 2 * slots * rows * TILE,
            transcendentals=rows * columns,
        ),
    )(plan, kept, came, focus_blocks)


def sum_kernel(place, chunks, label_ref, factor_ref, *refs):
    out_ref = refs[chunks]
    rows = refs[0].shape[1]
    out_ref[...] = jnp.zeros_like(out_ref)
    for sender in range(refs[0].shape[0] // CAP):
        for c in range(chunks):
            target = pl.ds(place(sender, c) * rows, rows)
            factor = factor_ref[target, sender : sender + 1]
            for r in range(CAP):
                slot = sender * CAP + r
                label = label_ref[slot]

                @pl.when(label >= 0)
                def _(slot=slot, label=label, target=target, factor=factor, c=c):
                    columns = pl.ds(pl.multiple_of(label * TILE, TILE), TILE)
                    out_ref[target, columns] += refs[c][slot].astype(jnp.float32) * factor


def sum_slots(labels, factor, received, place):
    rows = factor.shape[0]
    slots = received[0].shape[0]
    return pl.pallas_call(
        functools.partial(sum_kernel, place, len(received)),
        out_shape=jax.ShapeDtypeStruct((rows, STILES_DEV * TILE), jnp.float32),
        in_specs=[SMEM] + [VMEM] * (1 + len(received)),
        out_specs=VMEM,
        compiler_params=pltpu.CompilerParams(vmem_limit_bytes=32 << 20),
        cost_estimate=pl.CostEstimate(
            flops=2 * slots * rows * TILE,
            bytes_accessed=2 * slots * rows * TILE + 4 * rows * STILES_DEV * TILE,
            transcendentals=0,
        ),
    )(labels, factor, *received)


def slot_plan(focus_tiles):
    owner = focus_tiles[..., 1] // STILES_DEV
    index = jnp.arange(focus_tiles.shape[-2], dtype=jnp.int32)
    same = (owner[..., :, None] == owner[..., None, :]) & (index[None, :] < index[:, None])
    rank = jnp.sum(same.astype(jnp.int32), axis=-1)
    return owner, focus_tiles[..., 1] % STILES_DEV, rank


def arriving_labels(all_tiles, senders, me):
    owner, tile, rank = slot_plan(all_tiles.reshape(senders, -1, 2))
    slot = jnp.arange(CAP, dtype=jnp.int32)
    hit = (owner[:, None, :] == me) & (rank[:, None, :] == slot[None, :, None])
    return (jnp.sum(jnp.where(hit, tile[:, None, :] + 1, 0), axis=-1) - 1).reshape(-1)


def per_device(hidden_states, head_weight, focus_tiles, focus_blocks):
    vocab, hid = lax.axis_size("vocab"), lax.axis_size("hid")
    me, core = lax.axis_index("vocab"), lax.axis_index("hid")
    tiles_here = head_weight.shape[1] // TILE
    slots = vocab * CAP
    staged = vocab == 16 and hid == 2

    def swap(x, k):
        return lax.ppermute(x, "vocab", [(i, i ^ k) for i in range(vocab)])

    def dot(x):
        return jnp.dot(x, head_weight, preferred_element_type=jnp.float32)

    owner, _, rank = slot_plan(focus_tiles)
    turn = jnp.broadcast_to(me & 3 if staged else 0, rank.shape)
    plan = jnp.stack([focus_tiles[:, 0] - me * tiles_here, owner * CAP + rank, turn])
    labels = arriving_labels(lax.all_gather(focus_tiles, "vocab"), vocab, me)

    def exchange(kept, came, blocks):
        out, stats = map_rows(plan, kept, came, focus_blocks, slots, blocks)
        rows = out.shape[1]
        out = out.reshape(vocab, CAP * rows, TILE)
        arrived = lax.all_to_all(out, "vocab", split_axis=0, concat_axis=0, tiled=True)
        stats = lax.all_gather(stats[:, :2].T, "vocab")
        return arrived.reshape(slots, rows, TILE), stats

    if staged:

        def spread(x, first):
            beside, above = swap(x, 1), swap(x, 2)
            far = swap(beside, 2) if first else swap(above, 1)
            return jnp.concatenate([x, beside, above, far])

        def chunk(near, away):
            mine = (me >> 3) == core
            other = dot(jnp.where(mine, away, near))
            came = lax.ppermute(other, "hid", [(0, 1), (1, 0)])
            return exchange(dot(jnp.where(mine, near, away)), came, 4)

        away = swap(hidden_states, 8)
        one, one_stats = chunk(spread(hidden_states, True), spread(away, False))
        two, two_stats = chunk(spread(swap(hidden_states, 4), True), spread(swap(away, 4), False))
        odd = (jnp.arange(vocab, dtype=jnp.int32) >> 2 & 1)[:, None, None] == 1
        stats = jnp.where(
            odd,
            jnp.concatenate([two_stats, one_stats], axis=-1),
            jnp.concatenate([one_stats, two_stats], axis=-1),
        )
        received = [one, two]

        def place(sender, c):
            return (sender >> 2 & 1) ^ c
    else:
        gathered = lax.all_gather(hidden_states, "vocab", axis=0, tiled=True)
        logits = lax.psum_scatter(dot(gathered), "hid", scatter_dimension=0, tiled=True)
        arrived, stats = exchange(logits, jnp.zeros_like(logits), 1)
        received = [arrived]

        def place(sender, c):
            return c

    top, total = stats[:, 0], stats[:, 1]
    scale = jnp.exp(top - jnp.max(top, axis=0))
    student_size = STILES_DEV * TILE * vocab
    factor = scale * (student_size / jnp.sum(scale * total, axis=0))
    return sum_slots(labels, factor.T, received, place)


def solution(mesh):
    return jax.shard_map(
        per_device,
        mesh=mesh,
        in_specs=(P("vocab", "hid"), P("hid", "vocab"), P("vocab", None), P("vocab", None, None)),
        out_specs=P("hid", "vocab"),
        check_vma=False,
    )
```

```python
import functools

import jax
import jax.numpy as jnp
from jax import lax
from jax.experimental import pallas as pl
from jax.experimental.pallas import tpu as pltpu
from jax.sharding import PartitionSpec as P

TILE = 128
STILES_DEV = 12
CAP = 2
STATS = 16
LABEL_ROW = 6
VMEM = pl.BlockSpec(memory_space=pltpu.VMEM)
SMEM = pl.BlockSpec(memory_space=pltpu.SMEM)
ANY = pl.BlockSpec(memory_space=pl.ANY)


def kernel_params(megabytes):
    return pltpu.CompilerParams(vmem_limit_bytes=megabytes << 20)


def stack_kernel(places, *refs):
    out_ref = refs[-1]
    for ref, (row, column) in zip(refs, places):
        out_ref[row : row + ref.shape[0], column : column + ref.shape[1]] = ref[...]


def stack_rows(blocks, earlier=()):
    rows, columns = blocks[0].shape
    places = [(i * rows, 0) for i in range(4)] + [(3 * rows, columns // 2)] * (len(blocks) - 4)
    return pl.pallas_call(
        functools.partial(stack_kernel, places),
        out_shape=jax.ShapeDtypeStruct((4 * rows, columns), blocks[0].dtype),
        in_specs=[VMEM] * len(blocks) + [ANY] * len(earlier),
        out_specs=VMEM,
        compiler_params=kernel_params(16),
        cost_estimate=pl.CostEstimate(
            flops=0, bytes_accessed=16 * rows * columns, transcendentals=0
        ),
    )(*blocks, *earlier)


def softmax_kernel(blocks, choices, where_ref, *refs):
    out_ref, stats_ref = refs[-2:]
    for choice in range(choices):

        @pl.when(where_ref[0] == choice)
        def _(choice=choice):
            kept_ref, came_ref = refs[2 * choice : 2 * choice + 2]
            softmax_block(blocks, where_ref[1], kept_ref, came_ref, out_ref, stats_ref)


def softmax_block(blocks, turn, kept_ref, came_ref, out_ref, stats_ref):
    all_rows = kept_ref.shape[0]
    rows = all_rows // blocks
    lane = lax.broadcasted_iota(jnp.int32, (rows, TILE), 1)
    stats_ref[...] = jnp.zeros_like(stats_ref)
    for i in range(blocks):
        source = pl.ds(pl.multiple_of((turn ^ i) * rows, 8), rows)
        logits = kept_ref[source, :] + came_ref[source, :]
        top = jnp.max(logits, axis=1, keepdims=True)
        values = jnp.exp(logits - top)
        total = jnp.sum(values, axis=1, keepdims=True)
        rest = jnp.where(lane < 3, top, total)
        high = rest.astype(jnp.bfloat16).astype(jnp.float32)
        rest = rest - high
        middle = rest.astype(jnp.bfloat16).astype(jnp.float32)
        place = lane % 3
        pieces = jnp.where(place == 0, high, jnp.where(place == 1, middle, rest - middle))
        stats_ref[pl.ds(i * rows, rows), :] = jnp.where(lane < 6, pieces, 0.0)
        weights = values.astype(jnp.bfloat16)
        for t in range(kept_ref.shape[1] // TILE):
            out_ref[pl.ds(t * all_rows + i * rows, rows), :] = weights[:, t * TILE : (t + 1) * TILE]
    for half in range(2):
        pieces = stats_ref[half * TILE : (half + 1) * TILE, :].T[:8]
        stats_ref[half * 8 : (half + 1) * 8, :] = pieces
    out_ref[out_ref.shape[0] - STATS :, :] = stats_ref[:STATS, :].astype(jnp.bfloat16)


def softmax_tiles(where, choices, blocks, earlier=()):
    rows, columns = choices[0][0].shape
    logits = [x for choice in choices for x in choice]
    return pl.pallas_call(
        functools.partial(softmax_kernel, blocks, len(choices)),
        out_shape=jax.ShapeDtypeStruct((columns // TILE * rows + STATS, TILE), jnp.bfloat16),
        in_specs=[SMEM] + [VMEM] * len(logits) + [ANY] * len(earlier),
        out_specs=VMEM,
        scratch_shapes=[pltpu.VMEM((2 * TILE, TILE), jnp.float32)],
        compiler_params=kernel_params(32),
        cost_estimate=pl.CostEstimate(
            flops=4 * rows * columns, bytes_accessed=10 * rows * columns, transcendentals=rows * columns
        ),
    )(where, *logits, *earlier)


def focus_kernel(rows, me_ref, pair_ref, tiles_ref, focus_ref, out_ref, seen_ref):
    owners, entries = out_ref.shape[0], focus_ref.shape[0]
    first = me_ref[0] * ((tiles_ref.shape[0] - STATS) // rows)
    stats = tiles_ref[tiles_ref.shape[0] - STATS :, :]
    bottom = pl.ds(CAP * rows, STATS)
    for owner in range(owners):
        out_ref[owner, bottom, :] = stats
        seen_ref[owner] = 0
    row = lax.broadcasted_iota(jnp.int32, (STATS, TILE), 0)
    lane = lax.broadcasted_iota(jnp.int32, (STATS, TILE), 1)
    scale = (1 << 19) // STILES_DEV + 1

    @pl.loop(0, entries, unroll=min(entries, 16))
    def _(e):
        student = pair_ref[2 * e + 1]
        owner = student * scale >> 19
        rank = seen_ref[owner]
        seen_ref[owner] = rank + 1
        label = (student - owner * STILES_DEV + 1).astype(jnp.float32)
        mark = jnp.where((row == LABEL_ROW) & (lane == rank), label, 0.0).astype(jnp.bfloat16)
        out_ref[owner, bottom, :] += mark
        source = pl.ds(pl.multiple_of((pair_ref[2 * e] - first) * rows, 16), rows)
        term = jnp.dot(tiles_ref[source, :], focus_ref[e], preferred_element_type=jnp.float32)
        target = pl.ds(pl.multiple_of(rank * rows, 16), rows)
        out_ref[owner, target, :] = term.astype(jnp.bfloat16)


def focus_products(me, pairs, tiles, focus_blocks, rows, owners):
    entries = focus_blocks.shape[0]
    size = CAP * rows + STATS
    return pl.pallas_call(
        functools.partial(focus_kernel, rows),
        out_shape=jax.ShapeDtypeStruct((owners, size, TILE), jnp.bfloat16),
        in_specs=[SMEM, SMEM, VMEM, VMEM],
        out_specs=VMEM,
        scratch_shapes=[pltpu.SMEM((owners,), jnp.int32)],
        compiler_params=kernel_params(32),
        cost_estimate=pl.CostEstimate(
            flops=2 * entries * rows * TILE * TILE,
            bytes_accessed=4 * owners * size * TILE,
            transcendentals=0,
        ),
    )(me, pairs, tiles, focus_blocks)


def sum_kernel(senders, place, *refs):
    out_ref, level_ref, factor_ref, label_ref, sem = refs[-5:]
    chunks = len(refs) - 5
    rows = (refs[0].shape[1] - STATS) // CAP
    for s in range(senders):
        marks = refs[0][s, CAP * rows :, :].astype(jnp.float32)
        level_ref[2, s : s + 1, :TILE] = marks[LABEL_ROW : LABEL_ROW + 1]
    to_scalars = pltpu.make_async_copy(level_ref.at[2, :, :TILE], label_ref, sem)
    to_scalars.start()
    out_ref[...] = jnp.zeros_like(out_ref)
    for group in range(chunks):
        for s in range(senders):
            stats = refs[place(s, group)][s, CAP * rows :, :].astype(jnp.float32)
            for half in range(2):
                columns = pl.ds(half * TILE, TILE)
                for kind in range(2):
                    i = 8 * half + 3 * kind
                    value = stats[i : i + 1] + stats[i + 1 : i + 2] + stats[i + 2 : i + 3]
                    level_ref[kind, s : s + 1, columns] = value
        top, total = level_ref[0, :senders, :], level_ref[1, :senders, :]
        scale = jnp.exp(top - jnp.max(top, axis=0, keepdims=True))
        total = jnp.sum(scale * total, axis=0, keepdims=True)
        level_ref[0, :senders, :] = scale * (STILES_DEV * TILE * senders / total)
        factor_ref[...] = level_ref[0].T
        target = pl.ds(group * rows, rows)
        if group == 0:
            to_scalars.wait()
        for s in range(senders):
            for r in range(CAP):
                label = label_ref[s, r].astype(jnp.int32) - 1

                @pl.when(label >= 0)
                def _(s=s, r=r, label=label, target=target, group=group):
                    factor = factor_ref[:rows, s : s + 1]
                    columns = pl.ds(pl.multiple_of(label * TILE, TILE), TILE)
                    tile = refs[place(s, group)][s, r * rows : (r + 1) * rows, :]
                    out_ref[target, columns] += tile.astype(jnp.float32) * factor


def sum_slots(received, place):
    senders, size, _ = received[0].shape
    rows, chunks = (size - STATS) // CAP, len(received)
    return pl.pallas_call(
        functools.partial(sum_kernel, senders, place),
        out_shape=jax.ShapeDtypeStruct((rows * chunks, STILES_DEV * TILE), jnp.float32),
        in_specs=[VMEM] * chunks,
        out_specs=VMEM,
        scratch_shapes=[
            pltpu.VMEM((3, TILE, 2 * TILE), jnp.float32),
            pltpu.VMEM((2 * TILE, TILE), jnp.float32),
            pltpu.SMEM((TILE, TILE), jnp.float32),
            pltpu.SemaphoreType.DMA,
        ],
        compiler_params=kernel_params(40),
        cost_estimate=pl.CostEstimate(
            flops=2 * senders * chunks * CAP * rows * TILE,
            bytes_accessed=4 * rows * chunks * STILES_DEV * TILE,
            transcendentals=0,
        ),
    )(*received)


def hold_kernel(x_ref, earlier_ref, out_ref):
    out_ref[...] = x_ref[...]


def hold(x, earlier):
    return pl.pallas_call(
        hold_kernel,
        out_shape=jax.ShapeDtypeStruct(x.shape, x.dtype),
        in_specs=[VMEM, ANY],
        out_specs=VMEM,
        compiler_params=kernel_params(16),
    )(x, earlier)


def halves_kernel(left_ref, right_ref, *refs):
    left_out, right_out = refs[-2:]
    half = left_out.shape[1]
    left_out[...] = left_ref[:, :half]
    right_out[...] = right_ref[:, half:]


def halves(left, right, earlier):
    rows, columns = left.shape
    return pl.pallas_call(
        halves_kernel,
        out_shape=[jax.ShapeDtypeStruct((rows, columns // 2), left.dtype)] * 2,
        in_specs=[VMEM] * 2 + [ANY] * len(earlier),
        out_specs=[VMEM] * 2,
        compiler_params=kernel_params(16),
    )(left, right, *earlier)


def per_device(hidden_states, head_weight, focus_tiles, focus_blocks):
    vocab, hid = lax.axis_size("vocab"), lax.axis_size("hid")
    me, core = lax.axis_index("vocab"), lax.axis_index("hid")
    pairs = focus_tiles.reshape(-1)

    def swap(x, k):
        return lax.ppermute(x, "vocab", [(i, i ^ k) for i in range(vocab)])

    def dot(x):
        return jnp.dot(x, head_weight, preferred_element_type=jnp.float32)

    def exchange(weights, rows):
        sent = focus_products(me[None], pairs, weights, focus_blocks, rows, vocab)
        return lax.all_to_all(sent, "vocab", split_axis=0, concat_axis=0, tiled=True)

    if vocab == 16 and hid == 2:
        zero = hidden_states
        two = swap(zero, 8)
        zero_x, zero_y = swap(zero, 1), swap(zero, 2)
        zero_d = swap(zero_x, 2)
        two_x, two_y = swap(two, 1), swap(two, 2)
        to_near = [(2 * v + 1 - (v >> 3), 2 * v + (v >> 3)) for v in range(vocab)]
        to_away = [(b, a) for a, b in to_near]
        mine = (me >> 3) == core
        where = jnp.stack([mine.astype(jnp.int32), me & 3])

        def product(blocks, pairs, earlier=()):
            logits = dot(stack_rows(blocks, earlier))
            return logits, lax.ppermute(logits, ("vocab", "hid"), pairs)

        def chunk(near, away):
            near, away = jnp.concatenate(near), jnp.concatenate(away)
            other = dot(jnp.where(mine, away, near))
            came = lax.ppermute(other, "hid", [(0, 1), (1, 0)])
            kept = dot(jnp.where(mine, near, away))
            return softmax_tiles(where, [(kept, came)] * 2, 4)

        near = product([zero, zero_x, zero_y, zero_d], to_near)
        two_d, two_e = halves(two_x, two_y, (near[0],))
        two_d, two_e = swap(two_d, 2), swap(two_e, 1)
        two_all = [two, two_x, two_y, two_d, two_e]
        one, three = swap(hold(zero, two), 4), swap(two, 4)
        one_x, one_y = swap(one, 1), swap(one, 2)
        three_x, three_y = swap(three, 1), swap(three, 2)
        one_d, three_d = swap(one_x, 2), swap(three_y, 1)
        away = product(two_all, to_away, (one, three))
        first = softmax_tiles(where, [away, near], 4)
        second = chunk([one, one_x, one_y, one_d], [three, three_x, three_y, three_d])
        rows = 4 * zero.shape[0]
        received = [exchange(first, rows), exchange(second, rows)]

        def place(sender, group):
            return (sender >> 2 & 1) ^ group
    else:
        gathered = lax.all_gather(hidden_states, "vocab", axis=0, tiled=True)
        logits = lax.psum_scatter(dot(gathered), "hid", scatter_dimension=0, tiled=True)
        rows = logits.shape[0]
        where = jnp.zeros((2,), jnp.int32)
        weights = softmax_tiles(where, [(logits, jnp.zeros_like(logits))], 1)
        received = [exchange(weights, rows)]

        def place(sender, group):
            return group

    return sum_slots(received, place)


def solution(mesh):
    return jax.shard_map(
        per_device,
        mesh=mesh,
        in_specs=(P("vocab", "hid"), P("hid", "vocab"), P("vocab", None), P("vocab", None, None)),
        out_specs=P("hid", "vocab"),
        check_vma=False,
    )
```

```python
import functools

import jax
import jax.numpy as jnp
from jax import lax
from jax.experimental import pallas as pl
from jax.experimental.pallas import tpu as pltpu
from jax.sharding import PartitionSpec as P

TILE = 128
STILES_DEV = 12
CAP = 2
STATS = 16
LABEL_ROW = 6
VMEM = pl.BlockSpec(memory_space=pltpu.VMEM)
SMEM = pl.BlockSpec(memory_space=pltpu.SMEM)
ANY = pl.BlockSpec(memory_space=pl.ANY)


def kernel_params(megabytes):
    return pltpu.CompilerParams(vmem_limit_bytes=megabytes << 20)


def stack_kernel(places, *refs):
    out_ref = refs[-1]
    for ref, (row, column) in zip(refs, places):
        out_ref[row : row + ref.shape[0], column : column + ref.shape[1]] = ref[...]


def stack_rows(blocks, earlier=()):
    rows, columns = blocks[0].shape
    places = [(i * rows, 0) for i in range(4)] + [(3 * rows, columns // 2)] * (len(blocks) - 4)
    return pl.pallas_call(
        functools.partial(stack_kernel, places),
        out_shape=jax.ShapeDtypeStruct((4 * rows, columns), blocks[0].dtype),
        in_specs=[VMEM] * len(blocks) + [ANY] * len(earlier),
        out_specs=VMEM,
        compiler_params=kernel_params(16),
        cost_estimate=pl.CostEstimate(
            flops=0, bytes_accessed=16 * rows * columns, transcendentals=0
        ),
    )(*blocks, *earlier)


def softmax_kernel(blocks, choices, where_ref, *refs):
    out_ref, stats_ref = refs[-2:]
    for choice in range(choices):

        @pl.when(where_ref[0] == choice)
        def _(choice=choice):
            kept_ref, came_ref = refs[2 * choice : 2 * choice + 2]
            softmax_block(blocks, where_ref[1], kept_ref, came_ref, out_ref, stats_ref)


def softmax_block(blocks, turn, kept_ref, came_ref, out_ref, stats_ref):
    all_rows = kept_ref.shape[0]
    rows = all_rows // blocks
    lane = lax.broadcasted_iota(jnp.int32, (rows, TILE), 1)
    stats_ref[...] = jnp.zeros_like(stats_ref)
    for i in range(blocks):
        source = pl.ds(pl.multiple_of((turn ^ i) * rows, 8), rows)
        logits = kept_ref[source, :] + came_ref[source, :]
        top = jnp.max(logits, axis=1, keepdims=True)
        values = jnp.exp(logits - top)
        total = jnp.sum(values, axis=1, keepdims=True)
        rest = jnp.where(lane < 3, top, total)
        high = rest.astype(jnp.bfloat16).astype(jnp.float32)
        rest = rest - high
        middle = rest.astype(jnp.bfloat16).astype(jnp.float32)
        place = lane % 3
        pieces = jnp.where(place == 0, high, jnp.where(place == 1, middle, rest - middle))
        stats_ref[pl.ds(i * rows, rows), :] = jnp.where(lane < 6, pieces, 0.0)
        weights = values.astype(jnp.bfloat16)
        for t in range(kept_ref.shape[1] // TILE):
            out_ref[pl.ds(t * all_rows + i * rows, rows), :] = weights[:, t * TILE : (t + 1) * TILE]
    for half in range(2):
        pieces = stats_ref[half * TILE : (half + 1) * TILE, :].T[:8]
        stats_ref[half * 8 : (half + 1) * 8, :] = pieces
    out_ref[out_ref.shape[0] - STATS :, :] = stats_ref[:STATS, :].astype(jnp.bfloat16)


def softmax_tiles(where, choices, blocks, earlier=()):
    rows, columns = choices[0][0].shape
    logits = [x for choice in choices for x in choice]
    return pl.pallas_call(
        functools.partial(softmax_kernel, blocks, len(choices)),
        out_shape=jax.ShapeDtypeStruct((columns // TILE * rows + STATS, TILE), jnp.bfloat16),
        in_specs=[SMEM] + [VMEM] * len(logits) + [ANY] * len(earlier),
        out_specs=VMEM,
        scratch_shapes=[pltpu.VMEM((2 * TILE, TILE), jnp.float32)],
        compiler_params=kernel_params(32),
        cost_estimate=pl.CostEstimate(
            flops=4 * rows * columns, bytes_accessed=10 * rows * columns, transcendentals=rows * columns
        ),
    )(where, *logits, *earlier)


def focus_kernel(rows, me_ref, pair_ref, tiles_ref, focus_ref, out_ref, seen_ref):
    owners, entries = out_ref.shape[0], focus_ref.shape[0]
    first = me_ref[0] * ((tiles_ref.shape[0] - STATS) // rows)
    stats = tiles_ref[tiles_ref.shape[0] - STATS :, :]
    bottom = pl.ds(CAP * rows, STATS)
    for owner in range(owners):
        out_ref[owner, bottom, :] = stats
        seen_ref[owner] = 0
    row = lax.broadcasted_iota(jnp.int32, (STATS, TILE), 0)
    lane = lax.broadcasted_iota(jnp.int32, (STATS, TILE), 1)
    scale = (1 << 19) // STILES_DEV + 1

    @pl.loop(0, entries, unroll=min(entries, 16))
    def _(e):
        student = pair_ref[2 * e + 1]
        owner = student * scale >> 19
        rank = seen_ref[owner]
        seen_ref[owner] = rank + 1
        label = (student - owner * STILES_DEV + 1).astype(jnp.float32)
        mark = jnp.where((row == LABEL_ROW) & (lane == rank), label, 0.0).astype(jnp.bfloat16)
        out_ref[owner, bottom, :] += mark
        source = pl.ds(pl.multiple_of((pair_ref[2 * e] - first) * rows, 16), rows)
        term = jnp.dot(tiles_ref[source, :], focus_ref[e], preferred_element_type=jnp.float32)
        target = pl.ds(pl.multiple_of(rank * rows, 16), rows)
        out_ref[owner, target, :] = term.astype(jnp.bfloat16)


def focus_products(me, pairs, tiles, focus_blocks, rows, owners):
    entries = focus_blocks.shape[0]
    size = CAP * rows + STATS
    return pl.pallas_call(
        functools.partial(focus_kernel, rows),
        out_shape=jax.ShapeDtypeStruct((owners, size, TILE), jnp.bfloat16),
        in_specs=[SMEM, SMEM, VMEM, VMEM],
        out_specs=VMEM,
        scratch_shapes=[pltpu.SMEM((owners,), jnp.int32)],
        compiler_params=kernel_params(32),
        cost_estimate=pl.CostEstimate(
            flops=2 * entries * rows * TILE * TILE,
            bytes_accessed=4 * owners * size * TILE,
            transcendentals=0,
        ),
    )(me, pairs, tiles, focus_blocks)


def focus_each_kernel(rows, me_ref, pair_ref, tiles_ref, focus_ref, *refs):
    outs, seen_ref = refs[:-1], refs[-1]
    first = me_ref[0] * ((tiles_ref.shape[0] - STATS) // rows)
    stats = tiles_ref[tiles_ref.shape[0] - STATS :, :]
    bottom = pl.ds(CAP * rows, STATS)
    for o, out_ref in enumerate(outs):
        out_ref[bottom, :] = stats
        seen_ref[o] = 0
    row = lax.broadcasted_iota(jnp.int32, (STATS, TILE), 0)
    lane = lax.broadcasted_iota(jnp.int32, (STATS, TILE), 1)
    scale = (1 << 19) // STILES_DEV + 1

    @pl.loop(0, focus_ref.shape[0])
    def _(e):
        student = pair_ref[2 * e + 1]
        owner = student * scale >> 19
        here = owner ^ me_ref[0]
        rank = seen_ref[here]
        seen_ref[here] = rank + 1
        label = (student - owner * STILES_DEV + 1).astype(jnp.float32)
        mark = jnp.where((row == LABEL_ROW) & (lane == rank), label, 0.0).astype(jnp.bfloat16)
        source = pl.ds(pl.multiple_of((pair_ref[2 * e] - first) * rows, 16), rows)
        term = jnp.dot(tiles_ref[source, :], focus_ref[e], preferred_element_type=jnp.float32)
        term = term.astype(jnp.bfloat16)
        target = pl.ds(pl.multiple_of(rank * rows, 16), rows)
        for o, out_ref in enumerate(outs):

            @pl.when(here == o)
            def _(out_ref=out_ref):
                out_ref[bottom, :] += mark
                out_ref[target, :] = term


def focus_each(me, pairs, tiles, focus_blocks, rows, owners):
    size = CAP * rows + STATS
    return pl.pallas_call(
        functools.partial(focus_each_kernel, rows),
        out_shape=[jax.ShapeDtypeStruct((size, TILE), jnp.bfloat16)] * owners,
        in_specs=[SMEM, SMEM, VMEM, VMEM],
        out_specs=[VMEM] * owners,
        scratch_shapes=[pltpu.SMEM((owners,), jnp.int32)],
        compiler_params=kernel_params(32),
    )(me, pairs, tiles, focus_blocks)


def sum_kernel(senders, place, me_ref, *refs):
    *whole_refs, out_ref, level_ref, factor_ref, label_ref, sem = refs
    me = me_ref[0]
    chunks = []
    while whole_refs:
        if len(whole_refs[0].shape) == 3:
            whole = whole_refs.pop(0)
            chunks.append([whole.at[s ^ me] for s in range(senders)])
        else:
            chunks.append(whole_refs[:senders])
            del whole_refs[:senders]
    rows = (chunks[0][0].shape[0] - STATS) // CAP
    for s in range(senders):
        marks = chunks[0][s][CAP * rows :, :].astype(jnp.float32)
        level_ref[2, s : s + 1, :TILE] = marks[LABEL_ROW : LABEL_ROW + 1]
    to_scalars = pltpu.make_async_copy(level_ref.at[2, :, :TILE], label_ref, sem)
    to_scalars.start()
    out_ref[...] = jnp.zeros_like(out_ref)
    for group in range(len(chunks)):
        came = [chunks[place(s, group)][s] for s in range(senders)]
        for s in range(senders):
            stats = came[s][CAP * rows :, :].astype(jnp.float32)
            for half in range(2):
                columns = pl.ds(half * TILE, TILE)
                for kind in range(2):
                    i = 8 * half + 3 * kind
                    value = stats[i : i + 1] + stats[i + 1 : i + 2] + stats[i + 2 : i + 3]
                    level_ref[kind, s : s + 1, columns] = value
        top, total = level_ref[0, :senders, :], level_ref[1, :senders, :]
        scale = jnp.exp(top - jnp.max(top, axis=0, keepdims=True))
        total = jnp.sum(scale * total, axis=0, keepdims=True)
        level_ref[0, :senders, :] = scale * (STILES_DEV * TILE * senders / total)
        factor_ref[...] = level_ref[0].T
        target = pl.ds(pl.multiple_of((group ^ me_ref[1]) * rows, 8), rows)
        if group == 0:
            to_scalars.wait()
        for s in range(senders):
            for r in range(CAP):
                label = label_ref[s, r].astype(jnp.int32) - 1

                @pl.when(label >= 0)
                def _(s=s, r=r, label=label, target=target, tile_ref=came[s]):
                    factor = factor_ref[:rows, s : s + 1]
                    columns = pl.ds(pl.multiple_of(label * TILE, TILE), TILE)
                    tile = tile_ref[r * rows : (r + 1) * rows, :]
                    out_ref[target, columns] += tile.astype(jnp.float32) * factor


def sum_slots(me, senders, received, place):
    chunks = len(received)
    rows = ((received[0][0] if isinstance(received[0], list) else received[0]).shape[-2] - STATS) // CAP
    arrays = []
    for one in received:
        arrays += one if isinstance(one, list) else [one]
    return pl.pallas_call(
        functools.partial(sum_kernel, senders, place),
        out_shape=jax.ShapeDtypeStruct((rows * chunks, STILES_DEV * TILE), jnp.float32),
        in_specs=[SMEM] + [VMEM] * len(arrays),
        out_specs=VMEM,
        scratch_shapes=[
            pltpu.VMEM((3, TILE, 2 * TILE), jnp.float32),
            pltpu.VMEM((2 * TILE, TILE), jnp.float32),
            pltpu.SMEM((TILE, TILE), jnp.float32),
            pltpu.SemaphoreType.DMA,
        ],
        compiler_params=kernel_params(40),
        cost_estimate=pl.CostEstimate(
            flops=2 * senders * chunks * CAP * rows * TILE,
            bytes_accessed=4 * rows * chunks * STILES_DEV * TILE,
            transcendentals=0,
        ),
    )(me, *arrays)


def hold_kernel(x_ref, earlier_ref, out_ref):
    out_ref[...] = x_ref[...]


def hold(x, earlier):
    return pl.pallas_call(
        hold_kernel,
        out_shape=jax.ShapeDtypeStruct(x.shape, x.dtype),
        in_specs=[VMEM, ANY],
        out_specs=VMEM,
        compiler_params=kernel_params(16),
    )(x, earlier)


def halves_kernel(left_ref, right_ref, *refs):
    left_out, right_out = refs[-2:]
    half = left_out.shape[1]
    left_out[...] = left_ref[:, :half]
    right_out[...] = right_ref[:, half:]


def halves(left, right, earlier):
    rows, columns = left.shape
    return pl.pallas_call(
        halves_kernel,
        out_shape=[jax.ShapeDtypeStruct((rows, columns // 2), left.dtype)] * 2,
        in_specs=[VMEM] * 2 + [ANY] * len(earlier),
        out_specs=[VMEM] * 2,
        compiler_params=kernel_params(16),
    )(left, right, *earlier)


def per_device(hidden_states, head_weight, focus_tiles, focus_blocks):
    vocab, hid = lax.axis_size("vocab"), lax.axis_size("hid")
    me, core = lax.axis_index("vocab"), lax.axis_index("hid")
    pairs = focus_tiles.reshape(-1)

    def swap(x, k):
        return lax.ppermute(x, "vocab", [(i, i ^ k) for i in range(vocab)])

    def dot(x):
        return jnp.dot(x, head_weight, preferred_element_type=jnp.float32)

    def exchange(weights, rows):
        sent = focus_products(me[None], pairs, weights, focus_blocks, rows, vocab)
        return lax.all_to_all(sent, "vocab", split_axis=0, concat_axis=0, tiled=True)

    if vocab == 16 and hid == 2:
        zero = hidden_states
        two = swap(zero, 8)
        zero_x, zero_y = swap(zero, 1), swap(zero, 2)
        zero_d = swap(zero_x, 2)
        two_x, two_y = swap(two, 1), swap(two, 2)
        to_near = [(2 * v + 1 - (v >> 3), 2 * v + (v >> 3)) for v in range(vocab)]
        to_away = [(b, a) for a, b in to_near]
        mine = (me >> 3) == core
        where = jnp.stack([mine.astype(jnp.int32), me & 3])

        def product(blocks, pairs, earlier=()):
            logits = dot(stack_rows(blocks, earlier))
            return logits, lax.ppermute(logits, ("vocab", "hid"), pairs)

        def chunk(near, away):
            near, away = jnp.concatenate(near), jnp.concatenate(away)
            other = dot(jnp.where(mine, away, near))
            came = lax.ppermute(other, "hid", [(0, 1), (1, 0)])
            kept = dot(jnp.where(mine, near, away))
            return softmax_tiles(where, [(kept, came)] * 2, 4)

        near = product([zero, zero_x, zero_y, zero_d], to_near)
        two_d, two_e = halves(two_x, two_y, (near[0],))
        two_d, two_e = swap(two_d, 2), swap(two_e, 1)
        two_all = [two, two_x, two_y, two_d, two_e]
        one, three = swap(hold(zero, two), 4), swap(two, 4)
        one_x, one_y = swap(one, 1), swap(one, 2)
        three_x, three_y = swap(three, 1), swap(three, 2)
        one_d = swap(zero_d, 4)
        three_d = swap(jnp.concatenate([two_d, two_e], axis=1), 4)
        away = product(two_all, to_away, (one, three))
        first = softmax_tiles(where, [away, near], 4)
        second = chunk([one, one_x, one_y, one_d], [three, three_x, three_y, three_d])
        rows = 4 * zero.shape[0]
        sent = focus_each(me[None], pairs, second, focus_blocks, rows, vocab)
        came = [sent[0]] + [swap(sent[j], j) for j in range(1, vocab)]
        received = [exchange(first, rows), came]
        turn = jnp.stack([me, me >> 2 & 1])

        def place(sender, group):
            return (sender >> 2 & 1) ^ group
    else:
        gathered = lax.all_gather(hidden_states, "vocab", axis=0, tiled=True)
        logits = lax.psum_scatter(dot(gathered), "hid", scatter_dimension=0, tiled=True)
        rows = logits.shape[0]
        where = jnp.zeros((2,), jnp.int32)
        weights = softmax_tiles(where, [(logits, jnp.zeros_like(logits))], 1)
        received = [exchange(weights, rows)]
        turn = jnp.zeros((2,), jnp.int32)

        def place(sender, group):
            return group

    return sum_slots(turn, vocab, received, place)


def solution(mesh):
    return jax.shard_map(
        per_device,
        mesh=mesh,
        in_specs=(P("vocab", "hid"), P("hid", "vocab"), P("vocab", None), P("vocab", None, None)),
        out_specs=P("hid", "vocab"),
        check_vma=False,
    )
```

```python
import functools

import jax
import jax.numpy as jnp
from jax import lax
from jax.experimental import pallas as pl
from jax.experimental.pallas import tpu as pltpu
from jax.sharding import PartitionSpec as P

TILE = 128
STILES_DEV = 12
CAP = 2
STATS = 16
LABEL_ROW = 6
VMEM = pl.BlockSpec(memory_space=pltpu.VMEM)
SMEM = pl.BlockSpec(memory_space=pltpu.SMEM)
ANY = pl.BlockSpec(memory_space=pl.ANY)


def kernel_params(megabytes):
    return pltpu.CompilerParams(vmem_limit_bytes=megabytes << 20)


def stack_kernel(places, *refs):
    out_ref = refs[-1]
    for ref, (row, column) in zip(refs, places):
        out_ref[row : row + ref.shape[0], column : column + ref.shape[1]] = ref[...]


def stack_rows(blocks, earlier=()):
    rows, columns = blocks[0].shape
    places = [(i * rows, 0) for i in range(4)] + [(3 * rows, columns // 2)] * (len(blocks) - 4)
    return pl.pallas_call(
        functools.partial(stack_kernel, places),
        out_shape=jax.ShapeDtypeStruct((4 * rows, columns), blocks[0].dtype),
        in_specs=[VMEM] * len(blocks) + [ANY] * len(earlier),
        out_specs=VMEM,
        compiler_params=kernel_params(16),
        cost_estimate=pl.CostEstimate(
            flops=0, bytes_accessed=16 * rows * columns, transcendentals=0
        ),
    )(*blocks, *earlier)


def softmax_kernel(blocks, choices, where_ref, *refs):
    out_ref, stats_ref = refs[-2:]
    for choice in range(choices):

        @pl.when(where_ref[0] == choice)
        def _(choice=choice):
            kept_ref, came_ref = refs[2 * choice : 2 * choice + 2]
            softmax_block(blocks, where_ref[1], kept_ref, came_ref, out_ref, stats_ref)


def softmax_block(blocks, turn, kept_ref, came_ref, out_ref, stats_ref):
    all_rows = kept_ref.shape[0]
    rows = all_rows // blocks
    lane = lax.broadcasted_iota(jnp.int32, (rows, TILE), 1)
    stats_ref[...] = jnp.zeros_like(stats_ref)
    for i in range(blocks):
        source = pl.ds(pl.multiple_of((turn ^ i) * rows, 8), rows)
        logits = kept_ref[source, :] + came_ref[source, :]
        top = jnp.max(logits, axis=1, keepdims=True)
        values = jnp.exp(logits - top)
        total = jnp.sum(values, axis=1, keepdims=True)
        rest = jnp.where(lane < 3, top, total)
        high = rest.astype(jnp.bfloat16).astype(jnp.float32)
        rest = rest - high
        middle = rest.astype(jnp.bfloat16).astype(jnp.float32)
        place = lane % 3
        pieces = jnp.where(place == 0, high, jnp.where(place == 1, middle, rest - middle))
        stats_ref[pl.ds(i * rows, rows), :] = jnp.where(lane < 6, pieces, 0.0)
        weights = values.astype(jnp.bfloat16)
        for t in range(kept_ref.shape[1] // TILE):
            out_ref[pl.ds(t * all_rows + i * rows, rows), :] = weights[:, t * TILE : (t + 1) * TILE]
    for half in range(2):
        pieces = stats_ref[half * TILE : (half + 1) * TILE, :].T[:8]
        stats_ref[half * 8 : (half + 1) * 8, :] = pieces
    out_ref[out_ref.shape[0] - STATS :, :] = stats_ref[:STATS, :].astype(jnp.bfloat16)


def softmax_tiles(where, choices, blocks, earlier=()):
    rows, columns = choices[0][0].shape
    logits = [x for choice in choices for x in choice]
    return pl.pallas_call(
        functools.partial(softmax_kernel, blocks, len(choices)),
        out_shape=jax.ShapeDtypeStruct((columns // TILE * rows + STATS, TILE), jnp.bfloat16),
        in_specs=[SMEM] + [VMEM] * len(logits) + [ANY] * len(earlier),
        out_specs=VMEM,
        scratch_shapes=[pltpu.VMEM((2 * TILE, TILE), jnp.float32)],
        compiler_params=kernel_params(32),
        cost_estimate=pl.CostEstimate(
            flops=4 * rows * columns, bytes_accessed=10 * rows * columns, transcendentals=rows * columns
        ),
    )(where, *logits, *earlier)


def focus_kernel(rows, me_ref, pair_ref, tiles_ref, focus_ref, out_ref, seen_ref):
    owners, entries = out_ref.shape[0], focus_ref.shape[0]
    first = me_ref[0] * ((tiles_ref.shape[0] - STATS) // rows)
    stats = tiles_ref[tiles_ref.shape[0] - STATS :, :]
    bottom = pl.ds(CAP * rows, STATS)
    for owner in range(owners):
        out_ref[owner, bottom, :] = stats
        seen_ref[owner] = 0
    row = lax.broadcasted_iota(jnp.int32, (STATS, TILE), 0)
    lane = lax.broadcasted_iota(jnp.int32, (STATS, TILE), 1)
    scale = (1 << 19) // STILES_DEV + 1

    @pl.loop(0, entries, unroll=min(entries, 16))
    def _(e):
        student = pair_ref[2 * e + 1]
        owner = student * scale >> 19
        rank = seen_ref[owner]
        seen_ref[owner] = rank + 1
        label = (student - owner * STILES_DEV + 1).astype(jnp.float32)
        mark = jnp.where((row == LABEL_ROW) & (lane == rank), label, 0.0).astype(jnp.bfloat16)
        out_ref[owner, bottom, :] += mark
        source = pl.ds(pl.multiple_of((pair_ref[2 * e] - first) * rows, 16), rows)
        term = jnp.dot(tiles_ref[source, :], focus_ref[e], preferred_element_type=jnp.float32)
        target = pl.ds(pl.multiple_of(rank * rows, 16), rows)
        out_ref[owner, target, :] = term.astype(jnp.bfloat16)


def focus_products(me, pairs, tiles, focus_blocks, rows, owners):
    entries = focus_blocks.shape[0]
    size = CAP * rows + STATS
    return pl.pallas_call(
        functools.partial(focus_kernel, rows),
        out_shape=jax.ShapeDtypeStruct((owners, size, TILE), jnp.bfloat16),
        in_specs=[SMEM, SMEM, VMEM, VMEM],
        out_specs=VMEM,
        scratch_shapes=[pltpu.SMEM((owners,), jnp.int32)],
        compiler_params=kernel_params(32),
        cost_estimate=pl.CostEstimate(
            flops=2 * entries * rows * TILE * TILE,
            bytes_accessed=4 * owners * size * TILE,
            transcendentals=0,
        ),
    )(me, pairs, tiles, focus_blocks)


def focus_each_kernel(rows, me_ref, pair_ref, tiles_ref, focus_ref, *refs):
    outs, seen_ref = refs[:-1], refs[-1]
    first = me_ref[0] * ((tiles_ref.shape[0] - STATS) // rows)
    stats = tiles_ref[tiles_ref.shape[0] - STATS :, :]
    bottom = pl.ds(CAP * rows, STATS)
    for o, out_ref in enumerate(outs):
        out_ref[bottom, :] = stats
        seen_ref[o] = 0
    row = lax.broadcasted_iota(jnp.int32, (STATS, TILE), 0)
    lane = lax.broadcasted_iota(jnp.int32, (STATS, TILE), 1)
    scale = (1 << 19) // STILES_DEV + 1

    @pl.loop(0, focus_ref.shape[0])
    def _(e):
        student = pair_ref[2 * e + 1]
        owner = student * scale >> 19
        here = owner ^ me_ref[0]
        rank = seen_ref[here]
        seen_ref[here] = rank + 1
        label = (student - owner * STILES_DEV + 1).astype(jnp.float32)
        mark = jnp.where((row == LABEL_ROW) & (lane == rank), label, 0.0).astype(jnp.bfloat16)
        source = pl.ds(pl.multiple_of((pair_ref[2 * e] - first) * rows, 16), rows)
        term = jnp.dot(tiles_ref[source, :], focus_ref[e], preferred_element_type=jnp.float32)
        term = term.astype(jnp.bfloat16)
        target = pl.ds(pl.multiple_of(rank * rows, 16), rows)
        for o, out_ref in enumerate(outs):

            @pl.when(here == o)
            def _(out_ref=out_ref):
                out_ref[bottom, :] += mark
                out_ref[target, :] = term


def focus_each(me, pairs, tiles, focus_blocks, rows, owners):
    size = CAP * rows + STATS
    return pl.pallas_call(
        functools.partial(focus_each_kernel, rows),
        out_shape=[jax.ShapeDtypeStruct((size, TILE), jnp.bfloat16)] * owners,
        in_specs=[SMEM, SMEM, VMEM, VMEM],
        out_specs=[VMEM] * owners,
        scratch_shapes=[pltpu.SMEM((owners,), jnp.int32)],
        compiler_params=kernel_params(32),
    )(me, pairs, tiles, focus_blocks)


def sum_kernel(senders, place, me_ref, *refs):
    *whole_refs, out_ref, piece_ref, mark_ref, factor_ref, label_ref, sem = refs
    me = me_ref[0]
    chunks = []
    while whole_refs:
        if len(whole_refs[0].shape) == 3:
            whole = whole_refs.pop(0)
            chunks.append([whole.at[s ^ me] for s in range(senders)])
        else:
            chunks.append(whole_refs[:senders])
            del whole_refs[:senders]
    rows = (chunks[0][0].shape[0] - STATS) // CAP
    to_scalars = pltpu.make_async_copy(mark_ref, label_ref, sem)

    def take(came):
        for s in range(senders):
            stats = came[s][CAP * rows :, :].astype(jnp.float32)
            piece_ref[s, :, :TILE] = stats[:8]
            piece_ref[s, :, TILE:] = stats[8:]

    def three(first):
        return piece_ref[:, first, :] + piece_ref[:, first + 1, :] + piece_ref[:, first + 2, :]

    for group in range(len(chunks)):
        came = [chunks[place(s, group)][s] for s in range(senders)]

        @pl.when(pl.program_id(0) == group)
        def _(group=group, came=came):
            take(came)
            if group == 0:
                mark_ref[...] = piece_ref[:, LABEL_ROW, :TILE]
                to_scalars.start()
            out_ref[...] = jnp.zeros_like(out_ref)
            top, total = three(0), three(3)
            scale = jnp.exp(top - jnp.max(top, axis=0, keepdims=True))
            total = jnp.sum(scale * total, axis=0, keepdims=True)
            scale *= STILES_DEV * TILE * senders / total
            rest = jnp.zeros((TILE - senders, scale.shape[1]), jnp.float32)
            factor_ref[...] = jnp.concatenate([scale, rest]).T
            if group == 0:
                to_scalars.wait()
            for s in range(senders):
                add_slots(label_ref, s, 0, came[s], rows, lambda s=s: factor_ref[:rows, s : s + 1], out_ref)


def add_slots(label_ref, s, r, tile_ref, rows, factor, out_ref):
    label = label_ref[s, r].astype(jnp.int32) - 1

    @pl.when(label >= 0)
    def _():
        scale = jnp.broadcast_to(factor(), (rows, TILE))
        columns = pl.ds(pl.multiple_of(label * TILE, TILE), TILE)
        tile = tile_ref[r * rows : (r + 1) * rows, :].astype(jnp.float32)
        out_ref[:, columns] += tile * scale
        if r + 1 < CAP:
            add_slots(label_ref, s, r + 1, tile_ref, rows, lambda: scale, out_ref)


def sum_slots(me, senders, received, place):
    chunks = len(received)
    rows = ((received[0][0] if isinstance(received[0], list) else received[0]).shape[-2] - STATS) // CAP
    arrays = []
    for one in received:
        arrays += one if isinstance(one, list) else [one]
    whole = pl.BlockSpec(memory_space=pltpu.VMEM)
    return pl.pallas_call(
        functools.partial(sum_kernel, senders, place),
        out_shape=jax.ShapeDtypeStruct((rows * chunks, STILES_DEV * TILE), jnp.float32),
        grid_spec=pltpu.PrefetchScalarGridSpec(
            num_scalar_prefetch=1,
            grid=(chunks,),
            in_specs=[whole] * len(arrays),
            out_specs=pl.BlockSpec((rows, STILES_DEV * TILE), lambda group, me: (group ^ me[1], 0)),
            scratch_shapes=[
                pltpu.VMEM((senders, 8, 2 * TILE), jnp.float32),
                pltpu.VMEM((senders, TILE), jnp.float32),
                pltpu.VMEM((2 * TILE, TILE), jnp.float32),
                pltpu.SMEM((senders, TILE), jnp.float32),
                pltpu.SemaphoreType.DMA,
            ],
        ),
        compiler_params=kernel_params(40),
        cost_estimate=pl.CostEstimate(
            flops=2 * senders * chunks * CAP * rows * TILE,
            bytes_accessed=4 * rows * chunks * STILES_DEV * TILE,
            transcendentals=0,
        ),
    )(me, *arrays)


def hold_kernel(x_ref, earlier_ref, out_ref):
    out_ref[...] = x_ref[...]


def hold(x, earlier):
    return pl.pallas_call(
        hold_kernel,
        out_shape=jax.ShapeDtypeStruct(x.shape, x.dtype),
        in_specs=[VMEM, ANY],
        out_specs=VMEM,
        compiler_params=kernel_params(16),
    )(x, earlier)


def halves_kernel(left_ref, right_ref, *refs):
    left_out, right_out = refs[-2:]
    half = left_out.shape[1]
    left_out[...] = left_ref[:, :half]
    right_out[...] = right_ref[:, half:]


def halves(left, right, earlier):
    rows, columns = left.shape
    return pl.pallas_call(
        halves_kernel,
        out_shape=[jax.ShapeDtypeStruct((rows, columns // 2), left.dtype)] * 2,
        in_specs=[VMEM] * 2 + [ANY] * len(earlier),
        out_specs=[VMEM] * 2,
        compiler_params=kernel_params(16),
    )(left, right, *earlier)


def per_device(hidden_states, head_weight, focus_tiles, focus_blocks):
    vocab, hid = lax.axis_size("vocab"), lax.axis_size("hid")
    me, core = lax.axis_index("vocab"), lax.axis_index("hid")
    pairs = focus_tiles.reshape(-1)

    def swap(x, k):
        return lax.ppermute(x, "vocab", [(i, i ^ k) for i in range(vocab)])

    def dot(x):
        return jnp.dot(x, head_weight, preferred_element_type=jnp.float32)

    def exchange(weights, rows):
        sent = focus_products(me[None], pairs, weights, focus_blocks, rows, vocab)
        return lax.all_to_all(sent, "vocab", split_axis=0, concat_axis=0, tiled=True)

    if vocab == 16 and hid == 2:
        zero = hidden_states
        two = swap(zero, 8)
        zero_x, zero_y = swap(zero, 1), swap(zero, 2)
        zero_d = swap(zero_y, 1)
        two_x, two_y = swap(two, 1), swap(two, 2)
        to_near = [(2 * v + 1 - (v >> 3), 2 * v + (v >> 3)) for v in range(vocab)]
        to_away = [(b, a) for a, b in to_near]
        mine = (me >> 3) == core
        where = jnp.stack([mine.astype(jnp.int32), me & 3])

        def product(blocks, pairs, earlier=()):
            logits = dot(stack_rows(blocks, earlier))
            return logits, lax.ppermute(logits, ("vocab", "hid"), pairs)

        def chunk(near, away):
            near, away = jnp.concatenate(near), jnp.concatenate(away)
            other = dot(jnp.where(mine, away, near))
            came = lax.ppermute(other, "hid", [(0, 1), (1, 0)])
            kept = dot(jnp.where(mine, near, away))
            return softmax_tiles(where, [(kept, came)] * 2, 4)

        near = product([zero, zero_x, zero_y, zero_d], to_near)
        two_d, two_e = halves(two_x, two_y, (near[0],))
        two_d, two_e = swap(two_d, 2), swap(two_e, 1)
        two_all = [two, two_x, two_y, two_d, two_e]
        one, three = swap(hold(zero, two), 4), swap(two, 4)
        one_x, one_y = swap(one, 1), swap(one, 2)
        three_x, three_y = swap(three, 1), swap(three, 2)
        one_d = swap(zero_d, 4)
        three_d = swap(jnp.concatenate([two_d, two_e], axis=1), 4)
        away = product(two_all, to_away, (one, three))
        first = softmax_tiles(where, [away, near], 4)
        second = chunk([one, one_x, one_y, one_d], [three, three_x, three_y, three_d])
        rows = 4 * zero.shape[0]
        sent = focus_each(me[None], pairs, second, focus_blocks, rows, vocab)
        came = [sent[0]] + [swap(sent[j], j) for j in range(1, vocab)]
        received = [exchange(first, rows), came]
        turn = jnp.stack([me, me >> 2 & 1])

        def place(sender, group):
            return (sender >> 2 & 1) ^ group
    else:
        gathered = lax.all_gather(hidden_states, "vocab", axis=0, tiled=True)
        logits = lax.psum_scatter(dot(gathered), "hid", scatter_dimension=0, tiled=True)
        rows = logits.shape[0]
        where = jnp.zeros((2,), jnp.int32)
        weights = softmax_tiles(where, [(logits, jnp.zeros_like(logits))], 1)
        received = [exchange(weights, rows)]
        turn = jnp.zeros((2,), jnp.int32)

        def place(sender, group):
            return group

    return sum_slots(turn, vocab, received, place)


def solution(mesh):
    return jax.shard_map(
        per_device,
        mesh=mesh,
        in_specs=(P("vocab", "hid"), P("hid", "vocab"), P("vocab", None), P("vocab", None, None)),
        out_specs=P("hid", "vocab"),
        check_vma=False,
    )
```

```python
import functools

import jax
import jax.numpy as jnp
from jax import lax
from jax.experimental import pallas as pl
from jax.experimental.pallas import tpu as pltpu
from jax.sharding import PartitionSpec as P

TILE = 128
STILES_DEV = 12
CAP = 2
STATS = 16
LABEL_ROW = 6
SENT = (0, 4, 5, 6, 7, 1, 2, 3, 8, 12, 9, 13, 10, 14, 11, 15)
VMEM = pl.BlockSpec(memory_space=pltpu.VMEM)
SMEM = pl.BlockSpec(memory_space=pltpu.SMEM)
ANY = pl.BlockSpec(memory_space=pl.ANY)


def kernel_params(megabytes):
    return pltpu.CompilerParams(vmem_limit_bytes=megabytes << 20)


def stack_kernel(places, *refs):
    out_ref = refs[-1]
    for ref, (row, column) in zip(refs, places):
        out_ref[row : row + ref.shape[0], column : column + ref.shape[1]] = ref[...]


def stack_rows(blocks, earlier=()):
    rows, columns = blocks[0].shape
    places = [(i * rows, 0) for i in range(4)] + [(3 * rows, columns // 2)] * (len(blocks) - 4)
    return pl.pallas_call(
        functools.partial(stack_kernel, places),
        out_shape=jax.ShapeDtypeStruct((4 * rows, columns), blocks[0].dtype),
        in_specs=[VMEM] * len(blocks) + [ANY] * len(earlier),
        out_specs=VMEM,
        compiler_params=kernel_params(16),
        cost_estimate=pl.CostEstimate(
            flops=0, bytes_accessed=16 * rows * columns, transcendentals=0
        ),
    )(*blocks, *earlier)


def softmax_kernel(blocks, choices, where_ref, *refs):
    out_ref, stats_ref = refs[-2:]
    for choice in range(choices):

        @pl.when(where_ref[0] == choice)
        def _(choice=choice):
            kept_ref, came_ref = refs[2 * choice : 2 * choice + 2]
            softmax_block(blocks, where_ref[1], kept_ref, came_ref, out_ref, stats_ref)


def softmax_block(blocks, turn, kept_ref, came_ref, out_ref, stats_ref):
    all_rows = kept_ref.shape[0]
    rows = all_rows // blocks
    lane = lax.broadcasted_iota(jnp.int32, (rows, TILE), 1)
    stats_ref[...] = jnp.zeros_like(stats_ref)
    for i in range(blocks):
        source = pl.ds(pl.multiple_of((turn ^ i) * rows, 8), rows)
        logits = kept_ref[source, :] + came_ref[source, :]
        top = jnp.max(logits, axis=1, keepdims=True)
        values = jnp.exp(logits - top)
        total = jnp.sum(values, axis=1, keepdims=True)
        rest = jnp.where(lane < 3, top, total)
        high = rest.astype(jnp.bfloat16).astype(jnp.float32)
        rest = rest - high
        middle = rest.astype(jnp.bfloat16).astype(jnp.float32)
        place = lane % 3
        pieces = jnp.where(place == 0, high, jnp.where(place == 1, middle, rest - middle))
        stats_ref[pl.ds(i * rows, rows), :] = jnp.where(lane < 6, pieces, 0.0)
        weights = values.astype(jnp.bfloat16)
        for t in range(kept_ref.shape[1] // TILE):
            out_ref[pl.ds(t * all_rows + i * rows, rows), :] = weights[:, t * TILE : (t + 1) * TILE]
    for half in range(2):
        pieces = stats_ref[half * TILE : (half + 1) * TILE, :].T[:8]
        stats_ref[half * 8 : (half + 1) * 8, :] = pieces
    out_ref[out_ref.shape[0] - STATS :, :] = stats_ref[:STATS, :].astype(jnp.bfloat16)


def softmax_tiles(where, choices, blocks, earlier=()):
    rows, columns = choices[0][0].shape
    logits = [x for choice in choices for x in choice]
    return pl.pallas_call(
        functools.partial(softmax_kernel, blocks, len(choices)),
        out_shape=jax.ShapeDtypeStruct((columns // TILE * rows + STATS, TILE), jnp.bfloat16),
        in_specs=[SMEM] + [VMEM] * len(logits) + [ANY] * len(earlier),
        out_specs=VMEM,
        scratch_shapes=[pltpu.VMEM((2 * TILE, TILE), jnp.float32)],
        compiler_params=kernel_params(32),
        cost_estimate=pl.CostEstimate(
            flops=4 * rows * columns, bytes_accessed=10 * rows * columns, transcendentals=rows * columns
        ),
    )(where, *logits, *earlier)


def focus_kernel(rows, me_ref, pair_ref, tiles_ref, focus_ref, out_ref, seen_ref):
    owners, entries = out_ref.shape[0], focus_ref.shape[0]
    first = me_ref[0] * ((tiles_ref.shape[0] - STATS) // rows)
    stats = tiles_ref[tiles_ref.shape[0] - STATS :, :]
    bottom = pl.ds(CAP * rows, STATS)
    for owner in range(owners):
        out_ref[owner, bottom, :] = stats
        seen_ref[owner] = 0
    row = lax.broadcasted_iota(jnp.int32, (STATS, TILE), 0)
    lane = lax.broadcasted_iota(jnp.int32, (STATS, TILE), 1)
    scale = (1 << 19) // STILES_DEV + 1

    @pl.loop(0, entries, unroll=min(entries, 16))
    def _(e):
        student = pair_ref[2 * e + 1]
        owner = student * scale >> 19
        rank = seen_ref[owner]
        seen_ref[owner] = rank + 1
        label = (student - owner * STILES_DEV + 1).astype(jnp.float32)
        mark = jnp.where((row == LABEL_ROW) & (lane == rank), label, 0.0).astype(jnp.bfloat16)
        out_ref[owner, bottom, :] += mark
        source = pl.ds(pl.multiple_of((pair_ref[2 * e] - first) * rows, 16), rows)
        term = jnp.dot(tiles_ref[source, :], focus_ref[e], preferred_element_type=jnp.float32)
        target = pl.ds(pl.multiple_of(rank * rows, 16), rows)
        out_ref[owner, target, :] = term.astype(jnp.bfloat16)


def focus_products(me, pairs, tiles, focus_blocks, rows, owners):
    entries = focus_blocks.shape[0]
    size = CAP * rows + STATS
    return pl.pallas_call(
        functools.partial(focus_kernel, rows),
        out_shape=jax.ShapeDtypeStruct((owners, size, TILE), jnp.bfloat16),
        in_specs=[SMEM, SMEM, VMEM, VMEM],
        out_specs=VMEM,
        scratch_shapes=[pltpu.SMEM((owners,), jnp.int32)],
        compiler_params=kernel_params(32),
        cost_estimate=pl.CostEstimate(
            flops=2 * entries * rows * TILE * TILE,
            bytes_accessed=4 * owners * size * TILE,
            transcendentals=0,
        ),
    )(me, pairs, tiles, focus_blocks)


def focus_each_kernel(rows, me_ref, pair_ref, tiles_ref, focus_ref, *refs):
    outs, seen_ref = refs[:-1], refs[-1]
    first = me_ref[0] * ((tiles_ref.shape[0] - STATS) // rows)
    stats = tiles_ref[tiles_ref.shape[0] - STATS :, :]
    bottom = pl.ds(CAP * rows, STATS)
    for o, out_ref in enumerate(outs):
        out_ref[bottom, :] = stats
        seen_ref[o] = 0
    row = lax.broadcasted_iota(jnp.int32, (STATS, TILE), 0)
    lane = lax.broadcasted_iota(jnp.int32, (STATS, TILE), 1)
    scale = (1 << 19) // STILES_DEV + 1

    @pl.loop(0, focus_ref.shape[0])
    def _(e):
        student = pair_ref[2 * e + 1]
        owner = student * scale >> 19
        here = owner ^ me_ref[0]
        rank = seen_ref[here]
        seen_ref[here] = rank + 1
        label = (student - owner * STILES_DEV + 1).astype(jnp.float32)
        mark = jnp.where((row == LABEL_ROW) & (lane == rank), label, 0.0).astype(jnp.bfloat16)
        source = pl.ds(pl.multiple_of((pair_ref[2 * e] - first) * rows, 16), rows)
        term = jnp.dot(tiles_ref[source, :], focus_ref[e], preferred_element_type=jnp.float32)
        term = term.astype(jnp.bfloat16)
        target = pl.ds(pl.multiple_of(rank * rows, 16), rows)
        for o, out_ref in enumerate(outs):

            @pl.when(here == o)
            def _(out_ref=out_ref):
                out_ref[bottom, :] += mark
                out_ref[target, :] = term


def focus_each(me, pairs, tiles, focus_blocks, rows, owners):
    size = CAP * rows + STATS
    return pl.pallas_call(
        functools.partial(focus_each_kernel, rows),
        out_shape=[jax.ShapeDtypeStruct((size, TILE), jnp.bfloat16)] * owners,
        in_specs=[SMEM, SMEM, VMEM, VMEM],
        out_specs=[VMEM] * owners,
        scratch_shapes=[pltpu.SMEM((owners,), jnp.int32)],
        compiler_params=kernel_params(32),
    )(me, pairs, tiles, focus_blocks)


def sum_kernel(senders, place, me_ref, *refs):
    *whole_refs, out_ref, piece_ref, mark_ref, factor_ref, label_ref, sem = refs
    me = me_ref[0]
    chunks = []
    while whole_refs:
        if len(whole_refs[0].shape) == 3:
            whole = whole_refs.pop(0)
            chunks.append([whole.at[s ^ me] for s in range(senders)])
        else:
            chunks.append([whole_refs[SENT.index(s)] for s in range(senders)])
            del whole_refs[:senders]
    rows = (chunks[0][0].shape[0] - STATS) // CAP
    to_scalars = pltpu.make_async_copy(mark_ref, label_ref, sem)

    def take(came):
        for s in range(senders):
            stats = came[s][CAP * rows :, :].astype(jnp.float32)
            piece_ref[s, :, :TILE] = stats[:8]
            piece_ref[s, :, TILE:] = stats[8:]

    def three(first):
        return piece_ref[:, first, :] + piece_ref[:, first + 1, :] + piece_ref[:, first + 2, :]

    for group in range(len(chunks)):
        came = [chunks[place(s, group)][s] for s in range(senders)]

        @pl.when(pl.program_id(0) == group)
        def _(group=group, came=came):
            take(came)
            if group == 0:
                mark_ref[...] = piece_ref[:, LABEL_ROW, :TILE]
                to_scalars.start()
            out_ref[...] = jnp.zeros_like(out_ref)
            top, total = three(0), three(3)
            scale = jnp.exp(top - jnp.max(top, axis=0, keepdims=True))
            total = jnp.sum(scale * total, axis=0, keepdims=True)
            scale *= STILES_DEV * TILE * senders / total
            rest = jnp.zeros((TILE - senders, scale.shape[1]), jnp.float32)
            factor_ref[...] = jnp.concatenate([scale, rest]).T
            if group == 0:
                to_scalars.wait()
            for s in range(senders):
                add_slots(label_ref, s, 0, came[s], rows, lambda s=s: factor_ref[:rows, s : s + 1], out_ref)


def add_slots(label_ref, s, r, tile_ref, rows, factor, out_ref):
    label = label_ref[s, r].astype(jnp.int32) - 1

    @pl.when(label >= 0)
    def _():
        scale = jnp.broadcast_to(factor(), (rows, TILE))
        columns = pl.ds(pl.multiple_of(label * TILE, TILE), TILE)
        tile = tile_ref[r * rows : (r + 1) * rows, :].astype(jnp.float32)
        out_ref[:, columns] += tile * scale
        if r + 1 < CAP:
            add_slots(label_ref, s, r + 1, tile_ref, rows, lambda: scale, out_ref)


def sum_slots(me, senders, received, place):
    chunks = len(received)
    rows = ((received[0][0] if isinstance(received[0], list) else received[0]).shape[-2] - STATS) // CAP
    arrays = []
    for one in received:
        arrays += one if isinstance(one, list) else [one]
    whole = pl.BlockSpec(memory_space=pltpu.VMEM)
    return pl.pallas_call(
        functools.partial(sum_kernel, senders, place),
        out_shape=jax.ShapeDtypeStruct((rows * chunks, STILES_DEV * TILE), jnp.float32),
        grid_spec=pltpu.PrefetchScalarGridSpec(
            num_scalar_prefetch=1,
            grid=(chunks,),
            in_specs=[whole] * len(arrays),
            out_specs=pl.BlockSpec((rows, STILES_DEV * TILE), lambda group, me: (group ^ me[1], 0)),
            scratch_shapes=[
                pltpu.VMEM((senders, 8, 2 * TILE), jnp.float32),
                pltpu.VMEM((senders, TILE), jnp.float32),
                pltpu.VMEM((2 * TILE, TILE), jnp.float32),
                pltpu.SMEM((senders, TILE), jnp.float32),
                pltpu.SemaphoreType.DMA,
            ],
        ),
        compiler_params=kernel_params(40),
        cost_estimate=pl.CostEstimate(
            flops=2 * senders * chunks * CAP * rows * TILE,
            bytes_accessed=4 * rows * chunks * STILES_DEV * TILE,
            transcendentals=0,
        ),
    )(me, *arrays)


def hold_kernel(x_ref, earlier_ref, out_ref):
    out_ref[...] = x_ref[...]


def hold(x, earlier):
    return pl.pallas_call(
        hold_kernel,
        out_shape=jax.ShapeDtypeStruct(x.shape, x.dtype),
        in_specs=[VMEM, ANY],
        out_specs=VMEM,
        compiler_params=kernel_params(16),
    )(x, earlier)


def halves_kernel(left_ref, right_ref, *refs):
    left_out, right_out = refs[-2:]
    half = left_out.shape[1]
    left_out[...] = left_ref[:, :half]
    right_out[...] = right_ref[:, half:]


def halves(left, right, earlier):
    rows, columns = left.shape
    return pl.pallas_call(
        halves_kernel,
        out_shape=[jax.ShapeDtypeStruct((rows, columns // 2), left.dtype)] * 2,
        in_specs=[VMEM] * 2 + [ANY] * len(earlier),
        out_specs=[VMEM] * 2,
        compiler_params=kernel_params(16),
    )(left, right, *earlier)


def per_device(hidden_states, head_weight, focus_tiles, focus_blocks):
    vocab, hid = lax.axis_size("vocab"), lax.axis_size("hid")
    me, core = lax.axis_index("vocab"), lax.axis_index("hid")
    pairs = focus_tiles.reshape(-1)

    def swap(x, k):
        return lax.ppermute(x, "vocab", [(i, i ^ k) for i in range(vocab)])

    def dot(x):
        return jnp.dot(x, head_weight, preferred_element_type=jnp.float32)

    def exchange(weights, rows):
        sent = focus_products(me[None], pairs, weights, focus_blocks, rows, vocab)
        return lax.all_to_all(sent, "vocab", split_axis=0, concat_axis=0, tiled=True)

    if vocab == 16 and hid == 2:
        zero = hidden_states
        two = swap(zero, 8)
        held = hold(zero, focus_blocks)
        zero_x, zero_y = swap(held, 1), swap(zero, 2)
        zero_d = swap(zero_y, 1)
        two_x, two_y = swap(two, 1), swap(two, 2)
        to_near = [(2 * v + 1 - (v >> 3), 2 * v + (v >> 3)) for v in range(vocab)]
        to_away = [(b, a) for a, b in to_near]
        mine = (me >> 3) == core
        where = jnp.stack([mine.astype(jnp.int32), me & 3])

        def product(blocks, pairs, earlier=()):
            logits = dot(stack_rows(blocks, earlier))
            return logits, lax.ppermute(logits, ("vocab", "hid"), pairs)

        def chunk(near, away):
            near, away = jnp.concatenate(near), jnp.concatenate(away)
            other = dot(jnp.where(mine, away, near))
            came = lax.ppermute(other, "hid", [(0, 1), (1, 0)])
            kept = dot(jnp.where(mine, near, away))
            return softmax_tiles(where, [(kept, came)] * 2, 4)

        near = product([zero, zero_x, zero_y, zero_d], to_near)
        two_d, two_e = halves(two_x, two_y, (near[0],))
        two_d, two_e = swap(two_d, 2), swap(two_e, 1)
        two_all = [two, two_x, two_y, two_d, two_e]
        one, three = swap(hold(zero, two), 4), swap(two, 4)
        one_x, one_y = swap(one, 1), swap(one, 2)
        three_x, three_y = swap(three, 1), swap(three, 2)
        one_d = swap(zero_d, 4)
        three_d = swap(jnp.concatenate([two_d, two_e], axis=1), 4)
        away = product(two_all, to_away, (one, three))
        first = softmax_tiles(where, [away, near], 4)
        second = chunk([one, one_x, one_y, one_d], [three, three_x, three_y, three_d])
        rows = 4 * zero.shape[0]
        sent = focus_each(me[None], pairs, second, focus_blocks, rows, vocab)
        came = [swap(sent[j], j) if j else sent[j] for j in SENT]
        received = [exchange(first, rows), came]
        turn = jnp.stack([me, me >> 2 & 1])

        def place(sender, group):
            return (sender >> 2 & 1) ^ group
    else:
        gathered = lax.all_gather(hidden_states, "vocab", axis=0, tiled=True)
        logits = lax.psum_scatter(dot(gathered), "hid", scatter_dimension=0, tiled=True)
        rows = logits.shape[0]
        where = jnp.zeros((2,), jnp.int32)
        weights = softmax_tiles(where, [(logits, jnp.zeros_like(logits))], 1)
        received = [exchange(weights, rows)]
        turn = jnp.zeros((2,), jnp.int32)

        def place(sender, group):
            return group

    return sum_slots(turn, vocab, received, place)


def solution(mesh):
    return jax.shard_map(
        per_device,
        mesh=mesh,
        in_specs=(P("vocab", "hid"), P("hid", "vocab"), P("vocab", None), P("vocab", None, None)),
        out_specs=P("hid", "vocab"),
        check_vma=False,
    )
```

```python
import functools

import jax
import jax.numpy as jnp
from jax import lax
from jax.experimental import pallas as pl
from jax.experimental.pallas import tpu as pltpu
from jax.sharding import PartitionSpec as P

TILE = 128
STILES_DEV = 12
CAP = 2
STATS = 16
LABEL_ROW = 6
SENT = (0, 4, 5, 6, 7, 1, 2, 3, 8, 12, 9, 13, 10, 14, 11, 15)
VMEM = pl.BlockSpec(memory_space=pltpu.VMEM)
SMEM = pl.BlockSpec(memory_space=pltpu.SMEM)
ANY = pl.BlockSpec(memory_space=pl.ANY)


def kernel_params(megabytes):
    return pltpu.CompilerParams(vmem_limit_bytes=megabytes << 20)


def stack_kernel(places, *refs):
    out_ref = refs[-1]
    for ref, (row, column) in zip(refs, places):
        out_ref[row : row + ref.shape[0], column : column + ref.shape[1]] = ref[...]


def stack_rows(blocks, earlier=()):
    rows, columns = blocks[0].shape
    places = [(i * rows, 0) for i in range(4)] + [(3 * rows, columns // 2)] * (len(blocks) - 4)
    return pl.pallas_call(
        functools.partial(stack_kernel, places),
        out_shape=jax.ShapeDtypeStruct((4 * rows, columns), blocks[0].dtype),
        in_specs=[VMEM] * len(blocks) + [ANY] * len(earlier),
        out_specs=VMEM,
        compiler_params=kernel_params(10),
        cost_estimate=pl.CostEstimate(
            flops=0, bytes_accessed=16 * rows * columns, transcendentals=0
        ),
    )(*blocks, *earlier)


def softmax_kernel(blocks, choices, where_ref, *refs):
    out_ref, stats_ref = refs[-2:]
    for choice in range(choices):

        @pl.when(where_ref[0] == choice)
        def _(choice=choice):
            kept_ref, came_ref = refs[2 * choice : 2 * choice + 2]
            softmax_block(blocks, where_ref[1], kept_ref, came_ref, out_ref, stats_ref)


def softmax_block(blocks, turn, kept_ref, came_ref, out_ref, stats_ref):
    all_rows = kept_ref.shape[0]
    rows = all_rows // blocks
    lane = lax.broadcasted_iota(jnp.int32, (rows, TILE), 1)
    stats_ref[...] = jnp.zeros_like(stats_ref)
    for i in range(blocks):
        source = pl.ds(pl.multiple_of((turn ^ i) * rows, 8), rows)
        logits = kept_ref[source, :] + came_ref[source, :]
        top = jnp.max(logits, axis=1, keepdims=True)
        values = jnp.exp(logits - top)
        total = jnp.sum(values, axis=1, keepdims=True)
        rest = jnp.where(lane < 3, top, total)
        high = rest.astype(jnp.bfloat16).astype(jnp.float32)
        rest = rest - high
        middle = rest.astype(jnp.bfloat16).astype(jnp.float32)
        place = lane % 3
        pieces = jnp.where(place == 0, high, jnp.where(place == 1, middle, rest - middle))
        stats_ref[pl.ds(i * rows, rows), :] = jnp.where(lane < 6, pieces, 0.0)
        weights = values.astype(jnp.bfloat16)
        for t in range(kept_ref.shape[1] // TILE):
            out_ref[pl.ds(t * all_rows + i * rows, rows), :] = weights[:, t * TILE : (t + 1) * TILE]
    for half in range(2):
        pieces = stats_ref[half * TILE : (half + 1) * TILE, :].T[:8]
        stats_ref[half * 8 : (half + 1) * 8, :] = pieces
    out_ref[out_ref.shape[0] - STATS :, :] = stats_ref[:STATS, :].astype(jnp.bfloat16)


def softmax_tiles(where, choices, blocks, earlier=()):
    rows, columns = choices[0][0].shape
    logits = [x for choice in choices for x in choice]
    return pl.pallas_call(
        functools.partial(softmax_kernel, blocks, len(choices)),
        out_shape=jax.ShapeDtypeStruct((columns // TILE * rows + STATS, TILE), jnp.bfloat16),
        in_specs=[SMEM] + [VMEM] * len(logits) + [ANY] * len(earlier),
        out_specs=VMEM,
        scratch_shapes=[pltpu.VMEM((2 * TILE, TILE), jnp.float32)],
        compiler_params=kernel_params(20),
        cost_estimate=pl.CostEstimate(
            flops=4 * rows * columns, bytes_accessed=10 * rows * columns, transcendentals=rows * columns
        ),
    )(where, *logits, *earlier)


def focus_kernel(rows, me_ref, pair_ref, tiles_ref, focus_ref, out_ref, seen_ref):
    owners, entries = out_ref.shape[0], focus_ref.shape[0]
    first = me_ref[0] * ((tiles_ref.shape[0] - STATS) // rows)
    stats = tiles_ref[tiles_ref.shape[0] - STATS :, :]
    bottom = pl.ds(CAP * rows, STATS)
    for owner in range(owners):
        out_ref[owner, bottom, :] = stats
        seen_ref[owner] = 0
    row = lax.broadcasted_iota(jnp.int32, (STATS, TILE), 0)
    lane = lax.broadcasted_iota(jnp.int32, (STATS, TILE), 1)
    scale = (1 << 19) // STILES_DEV + 1

    @pl.loop(0, entries, unroll=min(entries, 16))
    def _(e):
        student = pair_ref[2 * e + 1]
        owner = student * scale >> 19
        rank = seen_ref[owner]
        seen_ref[owner] = rank + 1
        label = (student - owner * STILES_DEV + 1).astype(jnp.float32)
        mark = jnp.where((row == LABEL_ROW) & (lane == rank), label, 0.0).astype(jnp.bfloat16)
        out_ref[owner, bottom, :] += mark
        source = pl.ds(pl.multiple_of((pair_ref[2 * e] - first) * rows, 16), rows)
        term = jnp.dot(tiles_ref[source, :], focus_ref[e], preferred_element_type=jnp.float32)
        target = pl.ds(pl.multiple_of(rank * rows, 16), rows)
        out_ref[owner, target, :] = term.astype(jnp.bfloat16)


def focus_products(me, pairs, tiles, focus_blocks, rows, owners):
    entries = focus_blocks.shape[0]
    size = CAP * rows + STATS
    return pl.pallas_call(
        functools.partial(focus_kernel, rows),
        out_shape=jax.ShapeDtypeStruct((owners, size, TILE), jnp.bfloat16),
        in_specs=[SMEM, SMEM, VMEM, VMEM],
        out_specs=VMEM,
        scratch_shapes=[pltpu.SMEM((owners,), jnp.int32)],
        compiler_params=kernel_params(20),
        cost_estimate=pl.CostEstimate(
            flops=2 * entries * rows * TILE * TILE,
            bytes_accessed=4 * owners * size * TILE,
            transcendentals=0,
        ),
    )(me, pairs, tiles, focus_blocks)


def focus_each_kernel(rows, me_ref, pair_ref, tiles_ref, focus_ref, *refs):
    outs, seen_ref = refs[:-1], refs[-1]
    first = me_ref[0] * ((tiles_ref.shape[0] - STATS) // rows)
    stats = tiles_ref[tiles_ref.shape[0] - STATS :, :]
    bottom = pl.ds(CAP * rows, STATS)
    for o, out_ref in enumerate(outs):
        out_ref[bottom, :] = stats
        seen_ref[o] = 0
    row = lax.broadcasted_iota(jnp.int32, (STATS, TILE), 0)
    lane = lax.broadcasted_iota(jnp.int32, (STATS, TILE), 1)
    scale = (1 << 19) // STILES_DEV + 1

    @pl.loop(0, focus_ref.shape[0])
    def _(e):
        student = pair_ref[2 * e + 1]
        owner = student * scale >> 19
        here = owner ^ me_ref[0]
        rank = seen_ref[here]
        seen_ref[here] = rank + 1
        label = (student - owner * STILES_DEV + 1).astype(jnp.float32)
        mark = jnp.where((row == LABEL_ROW) & (lane == rank), label, 0.0).astype(jnp.bfloat16)
        source = pl.ds(pl.multiple_of((pair_ref[2 * e] - first) * rows, 16), rows)
        term = jnp.dot(tiles_ref[source, :], focus_ref[e], preferred_element_type=jnp.float32)
        term = term.astype(jnp.bfloat16)
        target = pl.ds(pl.multiple_of(rank * rows, 16), rows)
        for o, out_ref in enumerate(outs):

            @pl.when(here == o)
            def _(out_ref=out_ref):
                out_ref[bottom, :] += mark
                out_ref[target, :] = term


def focus_each(me, pairs, tiles, focus_blocks, rows, owners):
    size = CAP * rows + STATS
    return pl.pallas_call(
        functools.partial(focus_each_kernel, rows),
        out_shape=[jax.ShapeDtypeStruct((size, TILE), jnp.bfloat16)] * owners,
        in_specs=[SMEM, SMEM, VMEM, VMEM],
        out_specs=[VMEM] * owners,
        scratch_shapes=[pltpu.SMEM((owners,), jnp.int32)],
        compiler_params=kernel_params(20),
    )(me, pairs, tiles, focus_blocks)


def sum_kernel(senders, place, me_ref, *refs):
    *whole_refs, out_ref, piece_ref, mark_ref, factor_ref, label_ref, sem = refs
    me = me_ref[0]
    chunks = []
    while whole_refs:
        if len(whole_refs[0].shape) == 3:
            whole = whole_refs.pop(0)
            chunks.append([whole.at[s ^ me] for s in range(senders)])
        else:
            chunks.append([whole_refs[SENT.index(s)] for s in range(senders)])
            del whole_refs[:senders]
    rows = (chunks[0][0].shape[0] - STATS) // CAP
    to_scalars = pltpu.make_async_copy(mark_ref, label_ref, sem)

    def take(came):
        for s in range(senders):
            stats = came[s][CAP * rows :, :].astype(jnp.float32)
            piece_ref[s, :, :TILE] = stats[:8]
            piece_ref[s, :, TILE:] = stats[8:]

    def three(first):
        return piece_ref[:, first, :] + piece_ref[:, first + 1, :] + piece_ref[:, first + 2, :]

    for group in range(len(chunks)):
        came = [chunks[place(s, group)][s] for s in range(senders)]

        @pl.when(pl.program_id(0) == group)
        def _(group=group, came=came):
            take(came)
            if group == 0:
                mark_ref[...] = piece_ref[:, LABEL_ROW, :TILE]
                to_scalars.start()
            out_ref[...] = jnp.zeros_like(out_ref)
            top, total = three(0), three(3)
            scale = jnp.exp(top - jnp.max(top, axis=0, keepdims=True))
            total = jnp.sum(scale * total, axis=0, keepdims=True)
            scale *= STILES_DEV * TILE * senders / total
            rest = jnp.zeros((TILE - senders, scale.shape[1]), jnp.float32)
            factor_ref[...] = jnp.concatenate([scale, rest]).T
            if group == 0:
                to_scalars.wait()
            for s in range(senders):
                add_slots(label_ref, s, 0, came[s], rows, lambda s=s: factor_ref[:rows, s : s + 1], out_ref)


def add_slots(label_ref, s, r, tile_ref, rows, factor, out_ref):
    label = label_ref[s, r].astype(jnp.int32) - 1

    @pl.when(label >= 0)
    def _():
        scale = jnp.broadcast_to(factor(), (rows, TILE))
        columns = pl.ds(pl.multiple_of(label * TILE, TILE), TILE)
        tile = tile_ref[r * rows : (r + 1) * rows, :].astype(jnp.float32)
        out_ref[:, columns] += tile * scale
        if r + 1 < CAP:
            add_slots(label_ref, s, r + 1, tile_ref, rows, lambda: scale, out_ref)


def sum_slots(me, senders, received, place):
    chunks = len(received)
    rows = ((received[0][0] if isinstance(received[0], list) else received[0]).shape[-2] - STATS) // CAP
    arrays = []
    for one in received:
        arrays += one if isinstance(one, list) else [one]
    whole = pl.BlockSpec(memory_space=pltpu.VMEM)
    return pl.pallas_call(
        functools.partial(sum_kernel, senders, place),
        out_shape=jax.ShapeDtypeStruct((rows * chunks, STILES_DEV * TILE), jnp.float32),
        grid_spec=pltpu.PrefetchScalarGridSpec(
            num_scalar_prefetch=1,
            grid=(chunks,),
            in_specs=[whole] * len(arrays),
            out_specs=pl.BlockSpec((rows, STILES_DEV * TILE), lambda group, me: (group ^ me[1], 0)),
            scratch_shapes=[
                pltpu.VMEM((senders, 8, 2 * TILE), jnp.float32),
                pltpu.VMEM((senders, TILE), jnp.float32),
                pltpu.VMEM((2 * TILE, TILE), jnp.float32),
                pltpu.SMEM((senders, TILE), jnp.float32),
                pltpu.SemaphoreType.DMA,
            ],
        ),
        compiler_params=kernel_params(24),
        cost_estimate=pl.CostEstimate(
            flops=2 * senders * chunks * CAP * rows * TILE,
            bytes_accessed=4 * rows * chunks * STILES_DEV * TILE,
            transcendentals=0,
        ),
    )(me, *arrays)


def hold_kernel(x_ref, earlier_ref, out_ref):
    out_ref[...] = x_ref[...]


def hold(x, earlier):
    return pl.pallas_call(
        hold_kernel,
        out_shape=jax.ShapeDtypeStruct(x.shape, x.dtype),
        in_specs=[VMEM, ANY],
        out_specs=VMEM,
        compiler_params=kernel_params(10),
    )(x, earlier)


def halves_kernel(left_ref, right_ref, *refs):
    left_out, right_out = refs[-2:]
    half = left_out.shape[1]
    left_out[...] = left_ref[:, :half]
    right_out[...] = right_ref[:, half:]


def halves(left, right, earlier):
    rows, columns = left.shape
    return pl.pallas_call(
        halves_kernel,
        out_shape=[jax.ShapeDtypeStruct((rows, columns // 2), left.dtype)] * 2,
        in_specs=[VMEM] * 2 + [ANY] * len(earlier),
        out_specs=[VMEM] * 2,
        compiler_params=kernel_params(10),
    )(left, right, *earlier)


def per_device(hidden_states, head_weight, focus_tiles, focus_blocks):
    vocab, hid = lax.axis_size("vocab"), lax.axis_size("hid")
    me, core = lax.axis_index("vocab"), lax.axis_index("hid")
    pairs = focus_tiles.reshape(-1)

    def swap(x, k):
        return lax.ppermute(x, "vocab", [(i, i ^ k) for i in range(vocab)])

    def dot(x):
        return jnp.dot(x, head_weight, preferred_element_type=jnp.float32)

    def exchange(weights, rows):
        sent = focus_products(me[None], pairs, weights, focus_blocks, rows, vocab)
        return lax.all_to_all(sent, "vocab", split_axis=0, concat_axis=0, tiled=True)

    if vocab == 16 and hid == 2:
        zero = hidden_states
        two = swap(zero, 8)
        held = hold(zero, focus_blocks)
        zero_x, zero_y = swap(held, 1), swap(zero, 2)
        zero_d = swap(zero_y, 1)
        two_x, two_y = swap(two, 1), swap(two, 2)
        to_near = [(2 * v + 1 - (v >> 3), 2 * v + (v >> 3)) for v in range(vocab)]
        to_away = [(b, a) for a, b in to_near]
        mine = (me >> 3) == core
        where = jnp.stack([mine.astype(jnp.int32), me & 3])

        def product(blocks, pairs, earlier=()):
            logits = dot(stack_rows(blocks, earlier))
            return logits, lax.ppermute(logits, ("vocab", "hid"), pairs)

        def chunk(near, away):
            near, away = jnp.concatenate(near), jnp.concatenate(away)
            other = dot(jnp.where(mine, away, near))
            came = lax.ppermute(other, "hid", [(0, 1), (1, 0)])
            kept = dot(jnp.where(mine, near, away))
            return softmax_tiles(where, [(kept, came)] * 2, 4)

        near = product([zero, zero_x, zero_y, zero_d], to_near)
        two_d, two_e = halves(two_x, two_y, (near[0],))
        two_d, two_e = swap(two_d, 2), swap(two_e, 1)
        two_all = [two, two_x, two_y, two_d, two_e]
        one, three = swap(hold(zero, two), 4), swap(two, 4)
        one_x, one_y = swap(one, 1), swap(one, 2)
        three_x, three_y = swap(three, 1), swap(three, 2)
        one_d = swap(zero_d, 4)
        three_d = swap(jnp.concatenate([two_d, two_e], axis=1), 4)
        away = product(two_all, to_away, (one, three))
        first = softmax_tiles(where, [away, near], 4)
        second = chunk([one, one_x, one_y, one_d], [three, three_x, three_y, three_d])
        rows = 4 * zero.shape[0]
        sent = focus_each(me[None], pairs, second, focus_blocks, rows, vocab)
        came = [swap(sent[j], j) if j else sent[j] for j in SENT]
        received = [exchange(first, rows), came]
        turn = jnp.stack([me, me >> 2 & 1])

        def place(sender, group):
            return (sender >> 2 & 1) ^ group
    else:
        gathered = lax.all_gather(hidden_states, "vocab", axis=0, tiled=True)
        logits = lax.psum_scatter(dot(gathered), "hid", scatter_dimension=0, tiled=True)
        rows = logits.shape[0]
        where = jnp.zeros((2,), jnp.int32)
        weights = softmax_tiles(where, [(logits, jnp.zeros_like(logits))], 1)
        received = [exchange(weights, rows)]
        turn = jnp.zeros((2,), jnp.int32)

        def place(sender, group):
            return group

    return sum_slots(turn, vocab, received, place)


def solution(mesh):
    return jax.shard_map(
        per_device,
        mesh=mesh,
        in_specs=(P("vocab", "hid"), P("hid", "vocab"), P("vocab", None), P("vocab", None, None)),
        out_specs=P("hid", "vocab"),
        check_vma=False,
    )
```

```python
import functools

import jax
import jax.numpy as jnp
from jax import lax
from jax.experimental import pallas as pl
from jax.experimental.pallas import tpu as pltpu
from jax.sharding import PartitionSpec as P

TILE = 128
STILES_DEV = 12
CAP = 2
STATS = 16
LABEL_ROW = 6
SENT = (0, 4, 5, 6, 7, 1, 8, 12, 2, 9, 13, 3, 10, 14, 11, 15)
VMEM = pl.BlockSpec(memory_space=pltpu.VMEM)
SMEM = pl.BlockSpec(memory_space=pltpu.SMEM)
ANY = pl.BlockSpec(memory_space=pl.ANY)


def kernel_params(megabytes):
    return pltpu.CompilerParams(vmem_limit_bytes=megabytes << 20)


def stack_kernel(places, *refs):
    out_ref = refs[-1]
    for ref, (row, column) in zip(refs, places):
        out_ref[row : row + ref.shape[0], column : column + ref.shape[1]] = ref[...]


def stack_rows(blocks, earlier=()):
    rows, columns = blocks[0].shape
    places = [(i * rows, 0) for i in range(4)] + [(3 * rows, columns // 2)] * (len(blocks) - 4)
    return pl.pallas_call(
        functools.partial(stack_kernel, places),
        out_shape=jax.ShapeDtypeStruct((4 * rows, columns), blocks[0].dtype),
        in_specs=[VMEM] * len(blocks) + [ANY] * len(earlier),
        out_specs=VMEM,
        compiler_params=kernel_params(10),
        cost_estimate=pl.CostEstimate(
            flops=0, bytes_accessed=16 * rows * columns, transcendentals=0
        ),
    )(*blocks, *earlier)


def softmax_kernel(blocks, choices, where_ref, *refs):
    out_ref, stats_ref = refs[-2:]
    for choice in range(choices):

        @pl.when(where_ref[0] == choice)
        def _(choice=choice):
            kept_ref, came_ref = refs[2 * choice : 2 * choice + 2]
            softmax_block(blocks, where_ref[1], kept_ref, came_ref, out_ref, stats_ref)


def softmax_block(blocks, turn, kept_ref, came_ref, out_ref, stats_ref):
    all_rows = kept_ref.shape[0]
    rows = all_rows // blocks
    lane = lax.broadcasted_iota(jnp.int32, (rows, TILE), 1)
    stats_ref[...] = jnp.zeros_like(stats_ref)
    for i in range(blocks):
        source = pl.ds(pl.multiple_of((turn ^ i) * rows, 8), rows)
        logits = kept_ref[source, :] + came_ref[source, :]
        top = jnp.max(logits, axis=1, keepdims=True)
        values = jnp.exp(logits - top)
        total = jnp.sum(values, axis=1, keepdims=True)
        rest = jnp.where(lane < 3, top, total)
        high = rest.astype(jnp.bfloat16).astype(jnp.float32)
        rest = rest - high
        middle = rest.astype(jnp.bfloat16).astype(jnp.float32)
        place = lane % 3
        pieces = jnp.where(place == 0, high, jnp.where(place == 1, middle, rest - middle))
        stats_ref[pl.ds(i * rows, rows), :] = jnp.where(lane < 6, pieces, 0.0)
        weights = values.astype(jnp.bfloat16)
        for t in range(kept_ref.shape[1] // TILE):
            out_ref[pl.ds(t * all_rows + i * rows, rows), :] = weights[:, t * TILE : (t + 1) * TILE]
    for half in range(2):
        pieces = stats_ref[half * TILE : (half + 1) * TILE, :].T[:8]
        stats_ref[half * 8 : (half + 1) * 8, :] = pieces
    out_ref[out_ref.shape[0] - STATS :, :] = stats_ref[:STATS, :].astype(jnp.bfloat16)


def softmax_tiles(where, choices, blocks, earlier=()):
    rows, columns = choices[0][0].shape
    logits = [x for choice in choices for x in choice]
    return pl.pallas_call(
        functools.partial(softmax_kernel, blocks, len(choices)),
        out_shape=jax.ShapeDtypeStruct((columns // TILE * rows + STATS, TILE), jnp.bfloat16),
        in_specs=[SMEM] + [VMEM] * len(logits) + [ANY] * len(earlier),
        out_specs=VMEM,
        scratch_shapes=[pltpu.VMEM((2 * TILE, TILE), jnp.float32)],
        compiler_params=kernel_params(20),
        cost_estimate=pl.CostEstimate(
            flops=4 * rows * columns, bytes_accessed=10 * rows * columns, transcendentals=rows * columns
        ),
    )(where, *logits, *earlier)


def focus_kernel(rows, me_ref, pair_ref, tiles_ref, focus_ref, out_ref, seen_ref):
    owners, entries = out_ref.shape[0], focus_ref.shape[0]
    first = me_ref[0] * ((tiles_ref.shape[0] - STATS) // rows)
    stats = tiles_ref[tiles_ref.shape[0] - STATS :, :]
    bottom = pl.ds(CAP * rows, STATS)
    for owner in range(owners):
        out_ref[owner, bottom, :] = stats
        seen_ref[owner] = 0
    row = lax.broadcasted_iota(jnp.int32, (STATS, TILE), 0)
    lane = lax.broadcasted_iota(jnp.int32, (STATS, TILE), 1)
    scale = (1 << 19) // STILES_DEV + 1

    @pl.loop(0, entries, unroll=min(entries, 16))
    def _(e):
        student = pair_ref[2 * e + 1]
        owner = student * scale >> 19
        rank = seen_ref[owner]
        seen_ref[owner] = rank + 1
        label = (student - owner * STILES_DEV + 1).astype(jnp.float32)
        mark = jnp.where((row == LABEL_ROW) & (lane == rank), label, 0.0).astype(jnp.bfloat16)
        out_ref[owner, bottom, :] += mark
        source = pl.ds(pl.multiple_of((pair_ref[2 * e] - first) * rows, 16), rows)
        term = jnp.dot(tiles_ref[source, :], focus_ref[e], preferred_element_type=jnp.float32)
        target = pl.ds(pl.multiple_of(rank * rows, 16), rows)
        out_ref[owner, target, :] = term.astype(jnp.bfloat16)


def focus_products(me, pairs, tiles, focus_blocks, rows, owners):
    entries = focus_blocks.shape[0]
    size = CAP * rows + STATS
    return pl.pallas_call(
        functools.partial(focus_kernel, rows),
        out_shape=jax.ShapeDtypeStruct((owners, size, TILE), jnp.bfloat16),
        in_specs=[SMEM, SMEM, VMEM, VMEM],
        out_specs=VMEM,
        scratch_shapes=[pltpu.SMEM((owners,), jnp.int32)],
        compiler_params=kernel_params(20),
        cost_estimate=pl.CostEstimate(
            flops=2 * entries * rows * TILE * TILE,
            bytes_accessed=4 * owners * size * TILE,
            transcendentals=0,
        ),
    )(me, pairs, tiles, focus_blocks)


def focus_each_kernel(rows, me_ref, pair_ref, tiles_ref, focus_ref, *refs):
    outs, seen_ref = refs[:-1], refs[-1]
    first = me_ref[0] * ((tiles_ref.shape[0] - STATS) // rows)
    stats = tiles_ref[tiles_ref.shape[0] - STATS :, :]
    bottom = pl.ds(CAP * rows, STATS)
    for o, out_ref in enumerate(outs):
        out_ref[bottom, :] = stats
        seen_ref[o] = 0
    row = lax.broadcasted_iota(jnp.int32, (STATS, TILE), 0)
    lane = lax.broadcasted_iota(jnp.int32, (STATS, TILE), 1)
    scale = (1 << 19) // STILES_DEV + 1

    @pl.loop(0, focus_ref.shape[0])
    def _(e):
        student = pair_ref[2 * e + 1]
        owner = student * scale >> 19
        here = owner ^ me_ref[0]
        rank = seen_ref[here]
        seen_ref[here] = rank + 1
        label = (student - owner * STILES_DEV + 1).astype(jnp.float32)
        mark = jnp.where((row == LABEL_ROW) & (lane == rank), label, 0.0).astype(jnp.bfloat16)
        source = pl.ds(pl.multiple_of((pair_ref[2 * e] - first) * rows, 16), rows)
        term = jnp.dot(tiles_ref[source, :], focus_ref[e], preferred_element_type=jnp.float32)
        term = term.astype(jnp.bfloat16)
        target = pl.ds(pl.multiple_of(rank * rows, 16), rows)
        for o, out_ref in enumerate(outs):

            @pl.when(here == o)
            def _(out_ref=out_ref):
                out_ref[bottom, :] += mark
                out_ref[target, :] = term


def focus_each(me, pairs, tiles, focus_blocks, rows, owners):
    size = CAP * rows + STATS
    return pl.pallas_call(
        functools.partial(focus_each_kernel, rows),
        out_shape=[jax.ShapeDtypeStruct((size, TILE), jnp.bfloat16)] * owners,
        in_specs=[SMEM, SMEM, VMEM, VMEM],
        out_specs=[VMEM] * owners,
        scratch_shapes=[pltpu.SMEM((owners,), jnp.int32)],
        compiler_params=kernel_params(20),
    )(me, pairs, tiles, focus_blocks)


def sum_kernel(senders, place, me_ref, *refs):
    *whole_refs, out_ref, piece_ref, mark_ref, factor_ref, label_ref, sem = refs
    me = me_ref[0]
    chunks = []
    while whole_refs:
        if len(whole_refs[0].shape) == 3:
            whole = whole_refs.pop(0)
            chunks.append([whole.at[s ^ me] for s in range(senders)])
        else:
            chunks.append([whole_refs[SENT.index(s)] for s in range(senders)])
            del whole_refs[:senders]
    rows = (chunks[0][0].shape[0] - STATS) // CAP
    to_scalars = pltpu.make_async_copy(mark_ref, label_ref, sem)

    def take(came):
        for s in range(senders):
            stats = came[s][CAP * rows :, :].astype(jnp.float32)
            piece_ref[s, :, :TILE] = stats[:8]
            piece_ref[s, :, TILE:] = stats[8:]

    def three(first):
        return piece_ref[:, first, :] + piece_ref[:, first + 1, :] + piece_ref[:, first + 2, :]

    for group in range(len(chunks)):
        came = [chunks[place(s, group)][s] for s in range(senders)]

        @pl.when(pl.program_id(0) == group)
        def _(group=group, came=came):
            take(came)
            if group == 0:
                mark_ref[...] = piece_ref[:, LABEL_ROW, :TILE]
                to_scalars.start()
            out_ref[...] = jnp.zeros_like(out_ref)
            top, total = three(0), three(3)
            scale = jnp.exp(top - jnp.max(top, axis=0, keepdims=True))
            total = jnp.sum(scale * total, axis=0, keepdims=True)
            scale *= STILES_DEV * TILE * senders / total
            rest = jnp.zeros((TILE - senders, scale.shape[1]), jnp.float32)
            factor_ref[...] = jnp.concatenate([scale, rest]).T
            if group == 0:
                to_scalars.wait()
            for s in range(senders):
                add_slots(label_ref, s, 0, came[s], rows, lambda s=s: factor_ref[:rows, s : s + 1], out_ref)


def add_slots(label_ref, s, r, tile_ref, rows, factor, out_ref):
    label = label_ref[s, r].astype(jnp.int32) - 1

    @pl.when(label >= 0)
    def _():
        scale = jnp.broadcast_to(factor(), (rows, TILE))
        columns = pl.ds(pl.multiple_of(label * TILE, TILE), TILE)
        tile = tile_ref[r * rows : (r + 1) * rows, :].astype(jnp.float32)
        out_ref[:, columns] += tile * scale
        if r + 1 < CAP:
            add_slots(label_ref, s, r + 1, tile_ref, rows, lambda: scale, out_ref)


def sum_slots(me, senders, received, place):
    chunks = len(received)
    rows = ((received[0][0] if isinstance(received[0], list) else received[0]).shape[-2] - STATS) // CAP
    arrays = []
    for one in received:
        arrays += one if isinstance(one, list) else [one]
    whole = pl.BlockSpec(memory_space=pltpu.VMEM)
    return pl.pallas_call(
        functools.partial(sum_kernel, senders, place),
        out_shape=jax.ShapeDtypeStruct((rows * chunks, STILES_DEV * TILE), jnp.float32),
        grid_spec=pltpu.PrefetchScalarGridSpec(
            num_scalar_prefetch=1,
            grid=(chunks,),
            in_specs=[whole] * len(arrays),
            out_specs=pl.BlockSpec((rows, STILES_DEV * TILE), lambda group, me: (group ^ me[1], 0)),
            scratch_shapes=[
                pltpu.VMEM((senders, 8, 2 * TILE), jnp.float32),
                pltpu.VMEM((senders, TILE), jnp.float32),
                pltpu.VMEM((2 * TILE, TILE), jnp.float32),
                pltpu.SMEM((senders, TILE), jnp.float32),
                pltpu.SemaphoreType.DMA,
            ],
        ),
        compiler_params=kernel_params(24),
        cost_estimate=pl.CostEstimate(
            flops=2 * senders * chunks * CAP * rows * TILE,
            bytes_accessed=4 * rows * chunks * STILES_DEV * TILE,
            transcendentals=0,
        ),
    )(me, *arrays)


def hold_kernel(x_ref, earlier_ref, out_ref):
    out_ref[...] = x_ref[...]


def hold(x, earlier):
    return pl.pallas_call(
        hold_kernel,
        out_shape=jax.ShapeDtypeStruct(x.shape, x.dtype),
        in_specs=[VMEM, ANY],
        out_specs=VMEM,
        compiler_params=kernel_params(10),
    )(x, earlier)


def halves_kernel(left_ref, right_ref, *refs):
    left_out, right_out = refs[-2:]
    half = left_out.shape[1]
    left_out[...] = left_ref[:, :half]
    right_out[...] = right_ref[:, half:]


def halves(left, right, earlier):
    rows, columns = left.shape
    return pl.pallas_call(
        halves_kernel,
        out_shape=[jax.ShapeDtypeStruct((rows, columns // 2), left.dtype)] * 2,
        in_specs=[VMEM] * 2 + [ANY] * len(earlier),
        out_specs=[VMEM] * 2,
        compiler_params=kernel_params(10),
    )(left, right, *earlier)


def per_device(hidden_states, head_weight, focus_tiles, focus_blocks):
    vocab, hid = lax.axis_size("vocab"), lax.axis_size("hid")
    me, core = lax.axis_index("vocab"), lax.axis_index("hid")
    pairs = focus_tiles.reshape(-1)

    def swap(x, k):
        return lax.ppermute(x, "vocab", [(i, i ^ k) for i in range(vocab)])

    def dot(x):
        return jnp.dot(x, head_weight, preferred_element_type=jnp.float32)

    def exchange(weights, rows):
        sent = focus_products(me[None], pairs, weights, focus_blocks, rows, vocab)
        return lax.all_to_all(sent, "vocab", split_axis=0, concat_axis=0, tiled=True)

    if vocab == 16 and hid == 2:
        zero = hidden_states
        two = swap(zero, 8)
        held = hold(zero, focus_blocks)
        zero_x, zero_y = swap(held, 1), swap(zero, 2)
        zero_d = swap(zero_y, 1)
        two_x, two_y = swap(two, 1), swap(two, 2)
        to_near = [(2 * v + 1 - (v >> 3), 2 * v + (v >> 3)) for v in range(vocab)]
        to_away = [(b, a) for a, b in to_near]
        mine = (me >> 3) == core
        where = jnp.stack([mine.astype(jnp.int32), me & 3])

        def product(blocks, pairs, earlier=()):
            logits = dot(stack_rows(blocks, earlier))
            return logits, lax.ppermute(logits, ("vocab", "hid"), pairs)

        def chunk(near, away):
            near, away = jnp.concatenate(near), jnp.concatenate(away)
            other = dot(jnp.where(mine, away, near))
            came = lax.ppermute(other, "hid", [(0, 1), (1, 0)])
            kept = dot(jnp.where(mine, near, away))
            return softmax_tiles(where, [(kept, came)] * 2, 4)

        near = product([zero, zero_x, zero_y, zero_d], to_near)
        two_d, two_e = halves(two_x, two_y, (near[0],))
        two_d, two_e = swap(two_d, 2), swap(two_e, 1)
        two_all = [two, two_x, two_y, two_d, two_e]
        one, three = swap(hold(zero, two), 4), swap(two, 4)
        one_x, one_y = swap(one, 1), swap(one, 2)
        three_x, three_y = swap(three, 1), swap(three, 2)
        one_d = swap(zero_d, 4)
        three_d = swap(jnp.concatenate([two_d, two_e], axis=1), 4)
        away = product(two_all, to_away, (one, three))
        first = softmax_tiles(where, [away, near], 4)
        second = chunk([one, one_x, one_y, one_d], [three, three_x, three_y, three_d])
        rows = 4 * zero.shape[0]
        sent = focus_each(me[None], pairs, second, focus_blocks, rows, vocab)
        came = [swap(sent[j], j) if j else sent[j] for j in SENT]
        received = [exchange(first, rows), came]
        turn = jnp.stack([me, me >> 2 & 1])

        def place(sender, group):
            return (sender >> 2 & 1) ^ group
    else:
        gathered = lax.all_gather(hidden_states, "vocab", axis=0, tiled=True)
        logits = lax.psum_scatter(dot(gathered), "hid", scatter_dimension=0, tiled=True)
        rows = logits.shape[0]
        where = jnp.zeros((2,), jnp.int32)
        weights = softmax_tiles(where, [(logits, jnp.zeros_like(logits))], 1)
        received = [exchange(weights, rows)]
        turn = jnp.zeros((2,), jnp.int32)

        def place(sender, group):
            return group

    return sum_slots(turn, vocab, received, place)


def solution(mesh):
    return jax.shard_map(
        per_device,
        mesh=mesh,
        in_specs=(P("vocab", "hid"), P("hid", "vocab"), P("vocab", None), P("vocab", None, None)),
        out_specs=P("hid", "vocab"),
        check_vma=False,
    )
```
